256 devices in a mesh: clip: 32 (over x, z_hi, core), seq: 8 (over z_lo, y).
Axes of the slice: x: 4, y: 4, z: 8 (z_hi: 4, z_lo: 2; z = z_hi * 2 + z_lo), core: 2. Of those that a mesh axis runs over, the one named last changes fastest.
Arguments:
- enc_terms: bfloat16 [32, 8, 128, 4096], P('clip', 'seq'), may hold values from -4 to 4
- enc_resid: bfloat16 [32, 128, 4096], P('clip'), may hold values from -6 to 6
- norm_gain: float32 [4096], replicated, may hold values from 0.1 to 1.9
- key_weight: bfloat16 [4096, 5120], P('clip', 'seq'), may hold values from -0.09375 to 0.09375
- value_weight: bfloat16 [4096, 5120], P('clip', 'seq'), may hold values from -0.09375 to 0.09375
- queries: bfloat16 [32, 1024, 5120], P('clip', 'seq'), may hold values from -6 to 6
- out_grad: bfloat16 [32, 1024, 5120], P('clip', 'seq'), may hold values from -6 to 6
Outputs:
- query_grad: bfloat16 [32, 1024, 5120], P('clip', 'seq')
- key_weight_grad: float32 [4096, 5120], P('clip', 'seq')
- value_weight_grad: float32 [4096, 5120], P('clip', 'seq')
The draws below stay inside these ranges and needn't reach their ends.
All inputs are finite; a program needn't handle non-finite values.
Results may differ from the reference program's by a relative error of at most 0.034.
Values may be sent and summed in bfloat16 or wider, within the bound.
A program may use at most 64 MiB of HBM per device.

```python
import jax
import jax.numpy as jnp
from jax import lax

D = 4096
HEAD_DIM = 128
TEXT = 128
HD = 5120
VID = 1024
CLIPS = 32
N_SEQ = 8


def level_of(rng, extent, cuts, low, high):
    def one(axis_at, shards_of):
        steps = jax.random.uniform(jax.random.fold_in(jax.random.fold_in(rng, 6), axis_at), (shards_of,), jnp.float32, low / len(cuts), high / len(cuts))
        return jnp.repeat(jnp.exp(steps), extent[axis_at] // shards_of).reshape((-1,) + (1,) * (len(extent) - axis_at - 1))

    level = one(*cuts[0])
    for cut in cuts[1:]:
        level = level * one(*cut)
    return level


def scatter_about(own_key, extent, spread, most, split=(), held_as=jnp.bfloat16):
    values = jax.random.normal(own_key, extent, jnp.float32) * spread
    if len(split) > 0:
        values = level_of(own_key, extent, split, -0.22, 0.18) * values
    return jnp.clip(values, min=-most, max=most).astype(held_as)


def setup_inputs(seed: int = 0) -> dict:
    key_list = jax.random.split(jax.random.key(seed), 8)
    return {
        "enc_terms": scatter_about(key_list[0], (CLIPS, N_SEQ, TEXT, D), 0.5, 4.0, ((0, 32), (1, 8))),
        "enc_resid": scatter_about(key_list[1], (CLIPS, TEXT, D), 1.0, 6.0, ((0, 32),)),
        "norm_gain": jnp.clip(1.0 + 0.18 * jax.random.normal(key_list[2], (D,), jnp.float32), 0.1, 1.9),
        "key_weight": scatter_about(key_list[3], (D, HD), D ** -0.5, 0.09375, ((0, 32), (1, 8))),
        "value_weight": scatter_about(key_list[4], (D, HD), D ** -0.5, 0.09375, ((0, 32), (1, 8))),
        "queries": scatter_about(key_list[5], (CLIPS, VID, HD), 1.0, 6.0, ((0, 32), (1, 8))),
        "out_grad": scatter_about(key_list[6], (CLIPS, VID, HD), 1.0, 6.0, ((0, 32), (1, 8))),
    }


def normalize(hidden, gain):
    mean_sq = lax.optimization_barrier(jnp.mean(hidden * hidden, axis=-1, keepdims=True))
    return (hidden * lax.rsqrt(mean_sq + 1e-06) * gain).astype(jnp.bfloat16)

def attend(query_rows, grad_rows, keys, values):
    count = query_rows.shape[0]
    heads = keys.shape[1] // HEAD_DIM
    scale = HEAD_DIM ** (-0.5)
    q_heads = query_rows.reshape(count, heads, HEAD_DIM)
    g_heads = grad_rows.reshape(count, heads, HEAD_DIM)
    k_heads = keys.reshape(keys.shape[0], heads, HEAD_DIM)
    v_heads = values.reshape(values.shape[0], heads, HEAD_DIM)
    scores = jnp.einsum('nhd,thd->hnt', q_heads, k_heads, preferred_element_type=jnp.float32) * scale
    expo = jnp.exp(scores)
    probs = expo / lax.optimization_barrier(jnp.sum(expo, axis=-1, keepdims=True))
    probs_b = probs.astype(jnp.bfloat16)
    attn = jnp.einsum('hnt,thd->nhd', probs_b, v_heads, preferred_element_type=jnp.float32)
    delta = lax.optimization_barrier(jnp.sum(g_heads.astype(jnp.float32) * attn, axis=-1))
    dprobs = jnp.einsum('nhd,thd->hnt', g_heads, v_heads, preferred_element_type=jnp.float32)
    dscores = (probs * (dprobs - jnp.transpose(delta)[:, :, None])).astype(jnp.bfloat16)
    query_grad = jnp.einsum('hnt,thd->nhd', dscores, k_heads, preferred_element_type=jnp.float32) * scale
    key_grad = jnp.einsum('hnt,nhd->thd', dscores, q_heads, preferred_element_type=jnp.float32) * scale
    val_grad = jnp.einsum('hnt,nhd->thd', probs_b, g_heads, preferred_element_type=jnp.float32)
    width = heads * HEAD_DIM
    return (query_grad.astype(jnp.bfloat16).reshape(count, width), key_grad.reshape(keys.shape[0], width), val_grad.reshape(keys.shape[0], width))

def reference(enc_terms, enc_resid, norm_gain, key_weight, value_weight, queries, out_grad):
    enc_sum = lax.optimization_barrier(jnp.sum(enc_terms.astype(jnp.float32), axis=1))
    text = normalize(enc_resid.astype(jnp.float32) + enc_sum, norm_gain)

    def per_clip(carry, pieces):
        text_clip, query_rows, grad_rows = pieces
        keys = jnp.dot(text_clip, key_weight, preferred_element_type=jnp.float32).astype(jnp.bfloat16)
        values = jnp.dot(text_clip, value_weight, preferred_element_type=jnp.float32).astype(jnp.bfloat16)
        query_grad, key_grad, val_grad = attend(query_rows, grad_rows, keys, values)
        dims = (((0,), (0,)), ((), ()))
        key_term = lax.dot_general(text_clip, key_grad.astype(jnp.bfloat16), dims, preferred_element_type=jnp.float32)
        val_term = lax.dot_general(text_clip, val_grad.astype(jnp.bfloat16), dims, preferred_element_type=jnp.float32)
        key_term = lax.optimization_barrier(key_term.astype(jnp.bfloat16)).astype(jnp.float32)
        val_term = lax.optimization_barrier(val_term.astype(jnp.bfloat16)).astype(jnp.float32)
        return ((carry[0] + key_term, carry[1] + val_term), query_grad)
    start = (jnp.zeros((D, HD), jnp.float32), jnp.zeros((D, HD), jnp.float32))
    totals, query_grad = lax.scan(per_clip, start, (text, queries, out_grad))
    return (query_grad, totals[0], totals[1])
```

```python
import jax
import jax.numpy as jnp
from jax import lax
from jax.experimental import pallas as pl
from jax.experimental.pallas import tpu as pltpu
from jax.sharding import PartitionSpec as P

MESH = pl.DeviceIdType.MESH
HEAD = 128
F32 = jnp.float32
BF16 = jnp.bfloat16


def dot(a, b, ca, cb):
    return lax.dot_general(a, b, (((ca,), (cb,)), ((), ())), preferred_element_type=F32)


def each(start, stop, body):
    lax.fori_loop(start, stop, lambda i, c: (body(i), c)[1], 0)


def device(x, z, k, l, y):
    return ((x * 4 + z) * 2 + k, l * 4 + y)


def kernel(
    enc, resid, gain, key_w, val_w, queries, grads,
    out_q, out_k, out_v,
    enc_buf, res_buf, text16, text, w_own, w_all, kv_part, kv_recv, kv, q_buf, g_buf, qg_buf,
    pg_send, pg_own, pg_recv, gr_own, gr_all, dw_part, dw_recv,
    loc, e_s, e_r, t1_s, t1_r, t2_s, t2_r, t3_s, t3_r, w_s, w_r, kv_s, kv_r, kx_s, kx_r,
    qg_s, qg_r, px_s, px_r, oq_s, oq_r, ga_s, ga_r, dw_s, dw_r,
):
    clip, seq = lax.axis_index("clip"), lax.axis_index("seq")
    x, z, k = lax.div(clip, 8), lax.rem(lax.div(clip, 2), 4), lax.rem(clip, 2)
    l, y = lax.div(seq, 4), lax.rem(seq, 4)
    el, ek = 1 - l, 1 - k

    def seq_dev(j):
        return device(x, z, k, lax.div(j, 4), lax.rem(j, 4))

    def row_dev(e):
        return device(x, lax.div(e, 2), lax.rem(e, 2), l, y)

    def clip_dev(e):
        return device(lax.rem(e, 4), z, lax.div(e, 4), l, y)

    my_row, my_clip = z * 2 + k, k * 4 + x

    def remote(src, dst, s, r, where):
        return pltpu.make_async_remote_copy(
            src_ref=src, dst_ref=dst, send_sem=s, recv_sem=r, device_id=where, device_id_type=MESH
        )

    def local(src, dst, i):
        return pltpu.make_async_copy(src, dst, loc.at[i])

    local(enc.at[0, 0, pl.ds(pl.multiple_of(seq * 16, 16), 16)], enc_buf.at[seq], 0).start()
    local(resid.at[0, pl.ds(pl.multiple_of(seq * 16, 16), 16)], res_buf, 1).start()
    local(key_w, w_own.at[0], 2).start()
    local(val_w, w_own.at[1], 3).start()

    def own_qg(i, l2):
        src, dst = ((queries, q_buf), (grads, g_buf))[i]
        return local(
            src.at[0, :, pl.ds(pl.multiple_of((l2 * 4 + y) * 640, 128), 640)],
            dst.at[l2, pl.ds(pl.multiple_of(y * 128, 128), 128)],
            4 + 2 * i + l2,
        )

    for i in range(2):
        for l2 in range(2):
            own_qg(i, l2).start()

    bar = pltpu.get_barrier_semaphore()

    def greet(where):
        pl.semaphore_signal(bar, inc=1, device_id=where, device_id_type=MESH)

    each(1, 8, lambda o: greet(seq_dev(lax.rem(seq + o, 8))))
    each(1, 8, lambda o: greet(row_dev(lax.rem(my_row + o, 8))))
    each(1, 8, lambda o: greet(clip_dev(lax.rem(my_clip + o, 8))))
    pl.semaphore_wait(bar, 21)

    def enc_copy(j, slot):
        return remote(
            enc.at[0, 0, pl.ds(pl.multiple_of(j * 16, 16), 16)],
            enc_buf.at[slot], e_s.at[j], e_r.at[slot], seq_dev(j),
        )

    each(1, 8, lambda o: enc_copy(lax.rem(seq + o, 8), seq).start())

    local(key_w, w_own.at[0], 2).wait()
    local(val_w, w_own.at[1], 3).wait()

    def w_copy(e, slot):
        return remote(
            w_own.at[lax.rem(e, 2)], w_all.at[slot], w_s.at[e], w_r.at[slot], row_dev(e)
        )

    each(1, 8, lambda o: w_copy(lax.rem(my_row + o, 8), my_row).start())
    local(w_own.at[k], w_all.at[my_row], 8).start()

    local(enc.at[0, 0, pl.ds(pl.multiple_of(seq * 16, 16), 16)], enc_buf.at[seq], 0).wait()
    local(resid.at[0, pl.ds(pl.multiple_of(seq * 16, 16), 16)], res_buf, 1).wait()

    def enc_wait(o):
        j = lax.rem(seq + o, 8)
        enc_copy(j, j).wait_recv()

    each(1, 8, enc_wait)
    hidden = []
    total = jnp.zeros((16, 1), F32)
    for b in range(4):
        cols = pl.ds(b * 1024, 1024)
        h = enc_buf[0, :, cols].astype(F32)
        for s in range(1, 8):
            h = h + enc_buf[s, :, cols].astype(F32)
        h = h + res_buf[:, cols].astype(F32)
        total = total + jnp.sum(h * h, axis=1, keepdims=True)
        hidden.append(h)
    inv = lax.rsqrt(total * (1.0 / 4096.0) + 1e-06)
    for b in range(4):
        cols = pl.ds(b * 1024, 1024)
        text16[b] = (hidden[b] * inv * gain[:, cols]).astype(BF16)

    rows16 = pl.ds(pl.multiple_of(seq * 16, 16), 16)

    def t1_copy(x2, slot):
        return remote(
            text16.at[x2], text.at[k, slot, rows16], t1_s.at[x2], t1_r.at[slot], device(x2, z, k, l, y)
        )

    each(1, 4, lambda o: t1_copy(lax.rem(x + o, 4), x).start())
    local(text16.at[x], text.at[k, x, rows16], 9).start()
    local(text16.at[x], text.at[k, x, rows16], 9).wait()

    def t1_wait(o):
        x2 = lax.rem(x + o, 4)
        t1_copy(x2, x2).wait_recv()

    each(1, 4, t1_wait)

    def t2_copy(j, slot):
        part = text.at[k, :, pl.ds(pl.multiple_of(slot * 16, 16), 16)]
        return remote(part, part, t2_s.at[j], t2_r.at[slot], seq_dev(j))

    each(1, 8, lambda o: t2_copy(lax.rem(seq + o, 8), seq).start())

    def qg_copy(i, l2, y2, slot):
        src, dst = ((queries, q_buf), (grads, g_buf))[i]
        return remote(
            src.at[0, :, pl.ds(pl.multiple_of((l2 * 4 + y2) * 640, 128), 640)],
            dst.at[l2, pl.ds(pl.multiple_of(slot * 128, 128), 128)],
            qg_s.at[2 * i + l2, y2], qg_r.at[2 * i + l2, slot], device(x, z, k, l, y2),
        )

    def t2_wait(o):
        j = lax.rem(seq + o, 8)
        t2_copy(j, j).wait_recv()

    each(1, 8, t2_wait)

    t3 = remote(text.at[k], text.at[k], t3_s.at[0], t3_r.at[0], device(x, z, ek, l, y))
    t3.start()

    def qg_start(o):
        y2 = lax.rem(y + o, 4)
        for i in range(2):
            for l2 in range(2):
                qg_copy(i, l2, y2, y).start()

    each(1, 4, qg_start)

    local(w_own.at[k], w_all.at[my_row], 8).wait()

    def w_wait(o):
        e = lax.rem(my_row + o, 8)
        w_copy(e, e).wait_recv()

    each(1, 8, w_wait)

    def kv_copy(e, slot):
        a, b = lax.div(e, 4), lax.rem(e, 4)
        c, d = lax.div(slot, 4), lax.rem(slot, 4)
        return remote(
            kv_part.at[a, b], kv_recv.at[c, d], kv_s.at[e], kv_r.at[slot], clip_dev(e)
        )

    def project(core):
        t = text[core].reshape(512, 1024)
        for n in (0, 256, 512):
            size = min(256, 640 - n)
            acc = dot(t, w_all[:, :, n : n + size].reshape(1024, size), 1, 0)
            kv_part[core, :, :, n : n + size] = acc.astype(BF16).reshape(4, 128, size)

    project(k)
    each(1, 4, lambda o: kv_copy(k * 4 + lax.rem(x + o, 4), my_clip).start())
    local(kv_part.at[k, x], kv_recv.at[k, x], 10).start()
    remote(text.at[ek], text.at[ek], t3_s.at[0], t3_r.at[0], device(x, z, ek, l, y)).wait_recv()
    project(ek)
    each(0, 4, lambda o: kv_copy(ek * 4 + lax.rem(x + o, 4), my_clip).start())
    local(kv_part.at[k, x], kv_recv.at[k, x], 10).wait()

    def kv_wait(o):
        e = lax.rem(my_clip + o, 8)
        kv_copy(e, e).wait_recv()

    each(1, 8, kv_wait)
    for i in range(2):
        acc = kv_recv[i, 0].astype(F32)
        for b in range(1, 4):
            acc = acc + kv_recv[i, b].astype(F32)
        kv[l, i] = acc.astype(BF16)

    def kx_copy(slot):
        return remote(kv.at[slot], kv.at[slot], kx_s.at[0], kx_r.at[0], device(x, z, k, el, y))

    kx_copy(l).start()

    scale = HEAD ** (-0.5)

    def qg_wait(l2):
        def from_y(o):
            y2 = lax.rem(y + o, 4)
            for i in range(2):
                qg_copy(i, l2, y2, y2).wait_recv()

        for i in range(2):
            own_qg(i, l2).wait()
        each(1, 4, from_y)

    def head(l2, c, keep):
        cols = pl.ds(pl.multiple_of(c * HEAD, HEAD), HEAD)
        qh, gh = q_buf[l2, :, cols], g_buf[l2, :, cols]
        kh, vh = kv[l2, 0, :, cols], kv[l2, 1, :, cols]
        e = jnp.exp(dot(kh, qh, 1, 1) * scale)
        probs = e * (1.0 / jnp.sum(e, axis=0, keepdims=True))
        probs_b = probs.astype(BF16)
        dprobs = dot(vh, gh, 1, 1)
        delta = jnp.sum(probs_b.astype(F32) * dprobs, axis=0, keepdims=True)
        ds = (probs * (dprobs - delta)).astype(BF16)
        qg_buf[l2, :, cols] = (dot(ds, kh, 0, 0) * scale).astype(BF16)
        keep[0, :, cols] = (dot(ds, qh, 1, 0) * scale).astype(keep.dtype)
        keep[1, :, cols] = dot(probs_b, gh, 1, 0).astype(keep.dtype)

    def oq_copy(l2, y2, slot):
        return remote(
            qg_buf.at[l2, pl.ds(pl.multiple_of(y2 * 128, 128), 128)],
            out_q.at[0, :, pl.ds(pl.multiple_of((l2 * 4 + slot) * 640, 128), 640)],
            oq_s.at[l2, y2], oq_r.at[l2, slot], device(x, z, k, l, y2),
        )

    def oq_own(l2):
        return local(
            qg_buf.at[l2, pl.ds(pl.multiple_of(y * 128, 128), 128)],
            out_q.at[0, :, pl.ds(pl.multiple_of((l2 * 4 + y) * 640, 128), 640)],
            11 + l2,
        )

    qg_wait(0)
    qg_wait(1)
    kx_copy(el).wait_recv()
    each(0, 5, lambda c: head(el, c, pg_send))

    def px_copy():
        return remote(pg_send, pg_recv, px_s.at[0], px_r.at[0], device(x, z, k, el, y))

    px_copy().start()
    each(0, 5, lambda c: head(l, c, pg_own))
    px_copy().wait_recv()
    gr_own[...] = (pg_own[...] + pg_recv[...].astype(F32)).astype(BF16)

    def ga_copy(e, slot):
        c, d = lax.div(slot, 4), lax.rem(slot, 4)
        return remote(
            gr_own.at[lax.div(e, 4)], gr_all.at[c, d], ga_s.at[e], ga_r.at[slot], clip_dev(e)
        )

    each(1, 8, lambda o: ga_copy(lax.rem(my_clip + o, 8), my_clip).start())
    local(gr_own.at[k], gr_all.at[k, x], 13).start()

    def oq_start(o):
        for l2 in range(2):
            oq_copy(l2, lax.rem(y + o, 4), y).start()

    each(1, 4, oq_start)
    for l2 in range(2):
        oq_own(l2).start()

    local(gr_own.at[k], gr_all.at[k, x], 13).wait()

    def ga_wait(o):
        e = lax.rem(my_clip + o, 8)
        ga_copy(e, e).wait_recv()

    each(1, 8, ga_wait)

    def dw_copy(e, slot):
        c, d = lax.rem(slot, 2), lax.div(slot, 2)
        return remote(dw_part.at[e], dw_recv.at[c, d], dw_s.at[e], dw_r.at[slot], row_dev(e))

    def dw_step(o):
        z2 = lax.rem(z + o, 4)
        cols = pl.ds(pl.multiple_of(z2 * 256, 256), 256)
        t = text[:, :, :, cols].reshape(1024, 256)
        for n in (0, 256, 512):
            size = min(256, 640 - n)
            acc = dot(t, gr_all[:, :, :, n : n + size].reshape(1024, size), 0, 0)
            dw_part[pl.ds(z2 * 2, 2), :, n : n + size] = acc.astype(BF16).reshape(2, 128, size)

    def dw_send(o):
        dw_step(o)
        z2 = lax.rem(z + o, 4)
        for k2 in range(2):
            dw_copy(z2 * 2 + k2, my_row).start()

    each(1, 4, dw_send)
    dw_step(0)
    dw_copy(z * 2 + ek, my_row).start()
    local(dw_part.at[my_row], dw_recv.at[k, z], 14).start()
    local(dw_part.at[my_row], dw_recv.at[k, z], 14).wait()

    def dw_wait(o):
        e = lax.rem(my_row + o, 8)
        dw_copy(e, e).wait_recv()

    each(1, 8, dw_wait)
    for i, out in ((0, out_k), (1, out_v)):
        acc = dw_recv[i, 0].astype(F32)
        for b in range(1, 4):
            acc = acc + dw_recv[i, b].astype(F32)
        out[...] = acc

    def oq_wait(o):
        y2 = lax.rem(y + o, 4)
        for l2 in range(2):
            oq_copy(l2, y2, y2).wait_recv()
            oq_copy(l2, y2, y).wait_send()
            for i in range(2):
                qg_copy(i, l2, y2, y).wait_send()

    each(1, 4, oq_wait)
    for l2 in range(2):
        oq_own(l2).wait()

    def send_wait(o):
        j = lax.rem(seq + o, 8)
        enc_copy(j, seq).wait_send()
        t2_copy(j, seq).wait_send()
        e = lax.rem(my_row + o, 8)
        w_copy(e, my_row).wait_send()
        dw_copy(e, my_row).wait_send()
        e = lax.rem(my_clip + o, 8)
        kv_copy(e, my_clip).wait_send()
        ga_copy(e, my_clip).wait_send()

    each(1, 8, send_wait)
    each(1, 4, lambda o: t1_copy(lax.rem(x + o, 4), x).wait_send())
    t3.wait_send()
    kx_copy(l).wait_send()
    px_copy().wait_send()


def on_device(enc_terms, enc_resid, norm_gain, key_weight, value_weight, queries, out_grad):
    any_spec = pl.BlockSpec(memory_space=pl.ANY)
    vmem = pl.BlockSpec(memory_space=pltpu.VMEM)
    dma = pltpu.SemaphoreType.DMA
    scratch = [
        pltpu.VMEM((8, 16, 4096), BF16),
        pltpu.VMEM((16, 4096), BF16),
        pltpu.VMEM((4, 16, 1024), BF16),
        pltpu.VMEM((2, 4, 128, 1024), BF16),
        pltpu.VMEM((2, 128, 640), BF16),
        pltpu.VMEM((8, 128, 640), BF16),
        pltpu.VMEM((2, 4, 128, 640), BF16),
        pltpu.VMEM((2, 4, 128, 640), BF16),
        pltpu.VMEM((2, 2, 128, 640), BF16),
        pltpu.VMEM((2, 512, 640), BF16),
        pltpu.VMEM((2, 512, 640), BF16),
        pltpu.VMEM((2, 512, 640), BF16),
        pltpu.VMEM((2, 128, 640), BF16),
        pltpu.VMEM((2, 128, 640), F32),
        pltpu.VMEM((2, 128, 640), BF16),
        pltpu.VMEM((2, 128, 640), BF16),
        pltpu.VMEM((2, 4, 128, 640), BF16),
        pltpu.VMEM((8, 128, 640), BF16),
        pltpu.VMEM((2, 4, 128, 640), BF16),
        dma((15,)),
        dma((8,)), dma((8,)),
        dma((4,)), dma((4,)),
        dma((8,)), dma((8,)),
        dma((1,)), dma((1,)),
        dma((8,)), dma((8,)),
        dma((8,)), dma((8,)),
        dma((1,)), dma((1,)),
        dma((4, 4)), dma((4, 4)),
        dma((1,)), dma((1,)),
        dma((2, 4)), dma((2, 4)),
        dma((8,)), dma((8,)),
        dma((8,)), dma((8,)),
    ]
    return pl.pallas_call(
        kernel,
        out_shape=(
            jax.ShapeDtypeStruct(queries.shape, BF16),
            jax.ShapeDtypeStruct(key_weight.shape, F32),
            jax.ShapeDtypeStruct(value_weight.shape, F32),
        ),
        in_specs=[any_spec, any_spec, vmem, any_spec, any_spec, any_spec, any_spec],
        out_specs=(any_spec, vmem, vmem),
        scratch_shapes=scratch,
        compiler_params=pltpu.CompilerParams(
            collective_id=0, has_side_effects=True, vmem_limit_bytes=52 * 2**20
        ),
        cost_estimate=pl.CostEstimate(flops=4 * 10**9, bytes_accessed=10**7, transcendentals=655360),
    )(enc_terms, enc_resid, norm_gain.reshape(1, -1), key_weight, value_weight, queries, out_grad)


def solution(mesh):
    in_specs = (
        P("clip", "seq", None, None),
        P("clip", None, None),
        P(),
        P("clip", "seq"),
        P("clip", "seq"),
        P("clip", "seq", None),
        P("clip", "seq", None),
    )
    out_specs = (P("clip", "seq", None), P("clip", "seq"), P("clip", "seq"))
    return jax.shard_map(
        on_device, mesh=mesh, in_specs=in_specs, out_specs=out_specs, check_vma=False
    )
```

```python
import jax
import jax.numpy as jnp
from jax import lax
from jax.experimental import pallas as pl
from jax.experimental.pallas import tpu as pltpu
from jax.sharding import PartitionSpec as P

MESH = pl.DeviceIdType.MESH
HEAD = 128
F32 = jnp.float32
BF16 = jnp.bfloat16
CUTS = ((0, 256), (256, 640))


def dot(a, b, ca, cb):
    return lax.dot_general(a, b, (((ca,), (cb,)), ((), ())), preferred_element_type=F32)


def each(start, stop, body):
    lax.fori_loop(start, stop, lambda i, c: (body(i), c)[1], 0)


def device(x, z, k, l, y):
    return ((x * 4 + z) * 2 + k, l * 4 + y)


def kernel(
    enc, resid, gain, key_w, val_w, queries, grads,
    out_q, out_k, out_v,
    enc_buf, res_buf, ez_own, ez_recv, text32, text, text_t, w_own, w_all, kv_part, kv_recv, kv, q_buf, g_buf, qg_buf,
    pg_send, pg_own, pg_recv, gr_own, gr_all, dw_part, dw_recv,
    loc, e_s, e_r, ez_s, ez_r, t1_s, t1_r, t2_s, t2_r, t3_s, t3_r, w_s, w_r, kv_s, kv_r, kx_s, kx_r,
    qg_s, qg_r, px_s, px_r, oq_s, oq_r, ga_s, ga_r, dw_s, dw_r,
):
    clip, seq = lax.axis_index("clip"), lax.axis_index("seq")
    x, z, k = lax.div(clip, 8), lax.rem(lax.div(clip, 2), 4), lax.rem(clip, 2)
    l, y = lax.div(seq, 4), lax.rem(seq, 4)
    el, ek = 1 - l, 1 - k
    my_row, my_clip = z * 2 + k, k * 4 + x

    def y_dev(y2):
        return device(x, z, k, l, y2)

    def row_dev(e):
        return device(x, lax.div(e, 2), lax.rem(e, 2), l, y)

    def clip_dev(e):
        return device(lax.rem(e, 4), z, lax.div(e, 4), l, y)

    def others(n, me, body):
        each(1, n, lambda o: body(lax.rem(me + o, n)))

    def remote(src, dst, s, r, where):
        return pltpu.make_async_remote_copy(
            src_ref=src, dst_ref=dst, send_sem=s, recv_sem=r, device_id=where, device_id_type=MESH
        )

    def local(src, dst, i):
        return pltpu.make_async_copy(src, dst, loc.at[i])

    sends, arrivals = [], {}

    def arrive(name):
        for wait in arrivals.pop(name):
            wait()

    def flush():
        for name in list(arrivals):
            arrive(name)
        for wait in sends:
            wait()

    def group(name, n, me, copy):
        others(n, me, lambda e: copy(e, me).start())
        sends.append(lambda: others(n, me, lambda e: copy(e, me).wait_send()))
        arrivals[name] = [lambda: others(n, me, lambda e: copy(e, e).wait_recv())]

    def pair(name, copy, back):
        copy.start()
        sends.append(copy.wait_send)
        arrivals[name] = [back.wait_recv]

    def keep(name, copy):
        copy.start()
        arrivals.setdefault(name, []).append(copy.wait)

    def rows_of(i, n):
        return pl.ds(pl.multiple_of(i * n, n), n)

    def columns(j):
        return pl.ds(pl.multiple_of(j * 640, 128), 640)

    keep("enc", local(enc.at[0, 0, rows_of(y, 32)], enc_buf.at[y], 0))
    keep("resid", local(resid.at[0, rows_of(y, 32)], res_buf, 1))
    keep("w_own", local(key_w, w_own.at[0], 2))
    keep("w_own", local(val_w, w_own.at[1], 3))

    def qg_copy(i, l2, y2, slot):
        src, dst = ((queries, q_buf), (grads, g_buf))[i]
        return remote(
            src.at[0, :, columns(l2 * 4 + y2)], dst.at[l2, rows_of(slot, 128)],
            qg_s.at[i, l2, y2], qg_r.at[i, l2, slot], y_dev(y2),
        )

    def qg_own(i, l2):
        src, dst = ((queries, q_buf), (grads, g_buf))[i]
        return local(src.at[0, :, columns(l2 * 4 + y)], dst.at[l2, rows_of(y, 128)], 4 + 2 * i + l2)

    def qg_start(name, l2):
        group(name + "_q", 4, y, lambda y2, slot: qg_copy(0, l2, y2, slot))
        group(name + "_g", 4, y, lambda y2, slot: qg_copy(1, l2, y2, slot))

    for i in range(2):
        keep("mine", qg_own(i, 0))
        keep("mine", qg_own(i, 1))

    bar = pltpu.get_barrier_semaphore()

    def greet(where):
        pl.semaphore_signal(bar, inc=1, device_id=where, device_id_type=MESH)

    others(4, y, lambda e: greet(y_dev(e)))
    greet(device(x, z, k, el, y))
    others(8, my_row, lambda e: greet(row_dev(e)))
    others(8, my_clip, lambda e: greet(clip_dev(e)))
    pl.semaphore_wait(bar, 18)

    def enc_copy(y2, slot):
        return remote(
            enc.at[0, 0, rows_of(y2, 32)], enc_buf.at[slot], e_s.at[y2], e_r.at[slot], y_dev(y2)
        )

    group("enc_y", 4, y, enc_copy)

    arrive("w_own")

    def w_copy(e, slot):
        return remote(
            w_own.at[lax.rem(e, 2)], w_all.at[slot], w_s.at[e], w_r.at[slot], row_dev(e)
        )

    for o in (1, 3):
        for k2 in range(2):
            w_copy(lax.rem(z + o, 4) * 2 + k2, my_row).start()
    w_copy(z * 2 + ek, my_row).start()
    sends.append(lambda: others(8, my_row, lambda e: w_copy(e, my_row).wait_send()))
    arrivals["w"] = [lambda: others(8, my_row, lambda e: w_copy(e, e).wait_recv())]
    keep("w", local(w_own.at[k], w_all.at[my_row], 8))

    arrive("enc")
    arrive("resid")
    arrive("enc_y")
    for b in range(4):
        cols = pl.ds(b * 1024, 1024)
        part = enc_buf[0, :, cols].astype(F32)
        for s in range(1, 4):
            part = part + enc_buf[s, :, cols].astype(F32)
        ez_own[:, cols] = part.astype(BF16)
    ez = remote(ez_own, ez_recv, ez_s.at[0], ez_r.at[0], device(x, z, k, el, y))
    pair("ez", ez, ez)
    qg_start("own", l)
    arrive("ez")
    for k2 in range(2):
        w_copy(lax.rem(z + 2, 4) * 2 + k2, my_row).start()

    def hidden(b):
        cols = pl.ds(b * 1024, 1024)
        return (ez_own[:, cols].astype(F32) + ez_recv[:, cols].astype(F32)) + res_buf[:, cols].astype(F32)

    total = jnp.zeros((32, 1), F32)
    for b in range(4):
        h = hidden(b)
        total = total + jnp.sum(h * h, axis=1, keepdims=True)
    inv = lax.rsqrt(total * (1.0 / 4096.0) + 1e-06)
    for b in range(4):
        text32[b] = (hidden(b) * inv * gain[:, pl.ds(b * 1024, 1024)]).astype(BF16)

    def t1_copy(x2, slot):
        return remote(
            text32.at[x2], text.at[k, slot, rows_of(y, 32)], t1_s.at[x2], t1_r.at[slot], device(x2, z, k, l, y)
        )

    group("t1", 4, x, t1_copy)
    keep("t1", local(text32.at[x], text.at[k, x, rows_of(y, 32)], 9))
    arrive("t1")

    def t2_copy(y2, slot):
        part = text.at[k, :, rows_of(slot, 32)]
        return remote(part, part, t2_s.at[y2], t2_r.at[slot], y_dev(y2))

    group("t2", 4, y, t2_copy)
    arrive("t2")

    def t3_copy(core):
        return remote(text.at[core], text.at[core], t3_s.at[0], t3_r.at[0], device(x, z, ek, l, y))

    pair("t3", t3_copy(k), t3_copy(ek))
    qg_start("far", el)
    arrive("w")

    def kv_copy(c, e, slot):
        cols = pl.ds(CUTS[c][0], CUTS[c][1] - CUTS[c][0])
        return remote(
            kv_part.at[lax.div(e, 4), lax.rem(e, 4), :, cols],
            kv_recv.at[lax.div(slot, 4), lax.rem(slot, 4), :, cols],
            kv_s.at[c, e], kv_r.at[c, slot], clip_dev(e),
        )

    def project(core, c):
        lo, hi = CUTS[c]
        t = text[core].reshape(512, 1024)
        acc = dot(t, w_all[:, :, lo:hi].reshape(1024, hi - lo), 1, 0)
        kv_part[core, :, :, lo:hi] = acc.astype(BF16).reshape(4, 128, hi - lo)

    for c, (lo, hi) in enumerate(CUTS):
        cols = pl.ds(lo, hi - lo)
        project(k, c)
        others(4, x, lambda x2: kv_copy(c, k * 4 + x2, my_clip).start())
        keep(f"kv{c}", local(kv_part.at[k, x, :, cols], kv_recv.at[k, x, :, cols], 10 + c))
        if c == 0:
            arrive("t3")
        project(ek, c)
        each(0, 4, lambda o: kv_copy(c, ek * 4 + lax.rem(x + o, 4), my_clip).start())
        sends.append(lambda c=c: others(8, my_clip, lambda e: kv_copy(c, e, my_clip).wait_send()))
        arrivals[f"kv{c}"].append(lambda c=c: others(8, my_clip, lambda e: kv_copy(c, e, e).wait_recv()))

    def turn(z2):
        text_t[z2] = text[:, :, :, rows_of(z2, 256)].reshape(1024, 256).T

    each(0, 4, turn)

    def kx_copy(c, slot):
        part = kv.at[slot, :, :, pl.ds(CUTS[c][0], CUTS[c][1] - CUTS[c][0])]
        return remote(part, part, kx_s.at[c], kx_r.at[c], device(x, z, k, el, y))

    def gather_kv(c):
        lo, hi = CUTS[c]
        arrive(f"kv{c}")
        for i in range(2):
            acc = kv_recv[i, 0, :, lo:hi].astype(F32)
            for b in range(1, 4):
                acc = acc + kv_recv[i, b, :, lo:hi].astype(F32)
            kv[l, i, :, lo:hi] = acc.astype(BF16)
        pair(f"kx{c}", kx_copy(c, l), kx_copy(c, el))

    scale = HEAD ** (-0.5)

    def head(l2, c, keep):
        cols = pl.ds(pl.multiple_of(c * HEAD, HEAD), HEAD)
        qh, gh = q_buf[l2, :, cols], g_buf[l2, :, cols]
        kh, vh = kv[l2, 0, :, cols], kv[l2, 1, :, cols]
        e = jnp.exp(dot(kh, qh, 1, 1) * scale)
        probs = e * (1.0 / jnp.sum(e, axis=0, keepdims=True))
        probs_b = probs.astype(BF16)
        dprobs = dot(vh, gh, 1, 1)
        delta = jnp.sum(probs_b.astype(F32) * dprobs, axis=0, keepdims=True)
        ds = (probs * (dprobs - delta)).astype(BF16)
        qg_buf[l2, :, cols] = (dot(ds, kh, 0, 0) * scale).astype(BF16)
        keep[0, :, cols] = (dot(ds, qh, 1, 0) * scale).astype(keep.dtype)
        keep[1, :, cols] = dot(probs_b, gh, 1, 0).astype(keep.dtype)

    def heads(l2, c, keep):
        lo, hi = CUTS[c]
        each(lo // HEAD, hi // HEAD, lambda h: head(l2, h, keep))

    def px_start(c):
        lo, hi = CUTS[c]
        cols = pl.ds(lo, hi - lo)
        copy = remote(
            pg_send.at[:, :, cols], pg_recv.at[:, :, cols], px_s.at[c], px_r.at[c], device(x, z, k, el, y)
        )
        pair(f"px{c}", copy, copy)

    def oq_copy(l2, y2, slot):
        return remote(
            qg_buf.at[l2, rows_of(y2, 128)], out_q.at[0, :, columns(l2 * 4 + slot)],
            oq_s.at[l2, y2], oq_r.at[l2, slot], y_dev(y2),
        )

    def oq_start(name, l2, i):
        group(name, 4, y, lambda y2, slot: oq_copy(l2, y2, slot))
        keep(name, local(qg_buf.at[l2, rows_of(y, 128)], out_q.at[0, :, columns(l2 * 4 + y)], i))

    def ga_copy(c, e, slot):
        cols = pl.ds(CUTS[c][0], CUTS[c][1] - CUTS[c][0])
        return remote(
            gr_own.at[lax.div(e, 4), :, cols], gr_all.at[lax.div(slot, 4), lax.rem(slot, 4), :, cols],
            ga_s.at[c, e], ga_r.at[c, slot], clip_dev(e),
        )

    def ga_start(c):
        lo, hi = CUTS[c]
        cols = pl.ds(lo, hi - lo)
        arrive(f"px{c}")
        gr_own[:, :, lo:hi] = (pg_own[:, :, lo:hi] + pg_recv[:, :, lo:hi].astype(F32)).astype(BF16)
        group(f"ga{c}", 8, my_clip, lambda e, slot: ga_copy(c, e, slot))
        keep(f"ga{c}", local(gr_own.at[k, :, cols], gr_all.at[k, x, :, cols], 14 + c))

    def dw_copy(c, e, slot):
        cols = pl.ds(CUTS[c][0], CUTS[c][1] - CUTS[c][0])
        return remote(
            dw_part.at[e, :, cols], dw_recv.at[lax.rem(slot, 2), lax.div(slot, 2), :, cols],
            dw_s.at[c, e], dw_r.at[c, slot], row_dev(e),
        )

    def dw_start(c):
        lo, hi = CUTS[c]
        cols = pl.ds(lo, hi - lo)
        arrive(f"ga{c}")

        def step(z2):
            acc = dot(text_t[z2], gr_all[:, :, :, lo:hi].reshape(1024, hi - lo), 1, 0)
            dw_part[pl.ds(z2 * 2, 2), :, lo:hi] = acc.astype(BF16).reshape(2, 128, hi - lo)

        def step_send(z2):
            step(z2)
            for k2 in range(2):
                dw_copy(c, z2 * 2 + k2, my_row).start()

        others(4, z, step_send)
        step(z)
        dw_copy(c, z * 2 + ek, my_row).start()
        sends.append(lambda: others(8, my_row, lambda e: dw_copy(c, e, my_row).wait_send()))
        arrivals[f"dw{c}"] = [lambda: others(8, my_row, lambda e: dw_copy(c, e, e).wait_recv())]
        keep(f"dw{c}", local(dw_part.at[my_row, :, cols], dw_recv.at[k, z, :, cols], 16 + c))

    def dw_end(c):
        lo, hi = CUTS[c]
        arrive(f"dw{c}")
        for i, out in ((0, out_k), (1, out_v)):
            acc = dw_recv[i, 0, :, lo:hi].astype(F32)
            for b in range(1, 4):
                acc = acc + dw_recv[i, b, :, lo:hi].astype(F32)
            out[:, lo:hi] = acc

    gather_kv(0)
    arrive("mine")
    for i in "qg":
        arrive("own_" + i)
    heads(l, 0, pg_own)
    gather_kv(1)
    for i in "qg":
        arrive("far_" + i)
    arrive("kx0")
    heads(el, 0, pg_send)
    px_start(0)
    heads(l, 1, pg_own)
    oq_start("oq_own", l, 12)
    ga_start(0)
    arrive("kx1")
    heads(el, 1, pg_send)
    px_start(1)
    oq_start("oq_far", el, 13)
    dw_start(0)
    ga_start(1)
    dw_start(1)
    dw_end(0)
    dw_end(1)
    flush()


def on_device(enc_terms, enc_resid, norm_gain, key_weight, value_weight, queries, out_grad):
    any_spec = pl.BlockSpec(memory_space=pl.ANY)
    vmem = pl.BlockSpec(memory_space=pltpu.VMEM)
    dma = pltpu.SemaphoreType.DMA
    scratch = [
        pltpu.VMEM((4, 32, 4096), BF16),
        pltpu.VMEM((32, 4096), BF16),
        pltpu.VMEM((32, 4096), BF16),
        pltpu.VMEM((32, 4096), BF16),
        pltpu.VMEM((4, 32, 1024), BF16),
        pltpu.VMEM((2, 4, 128, 1024), BF16),
        pltpu.VMEM((4, 256, 1024), BF16),
        pltpu.VMEM((2, 128, 640), BF16),
        pltpu.VMEM((8, 128, 640), BF16),
        pltpu.VMEM((2, 4, 128, 640), BF16),
        pltpu.VMEM((2, 4, 128, 640), BF16),
        pltpu.VMEM((2, 2, 128, 640), BF16),
        pltpu.VMEM((2, 512, 640), BF16),
        pltpu.VMEM((2, 512, 640), BF16),
        pltpu.VMEM((2, 512, 640), BF16),
        pltpu.VMEM((2, 128, 640), BF16),
        pltpu.VMEM((2, 128, 640), F32),
        pltpu.VMEM((2, 128, 640), BF16),
        pltpu.VMEM((2, 128, 640), BF16),
        pltpu.VMEM((2, 4, 128, 640), BF16),
        pltpu.VMEM((8, 128, 640), BF16),
        pltpu.VMEM((2, 4, 128, 640), BF16),
        dma((18,)),
        dma((4,)), dma((4,)),
        dma((1,)), dma((1,)),
        dma((4,)), dma((4,)),
        dma((4,)), dma((4,)),
        dma((1,)), dma((1,)),
        dma((8,)), dma((8,)),
        dma((2, 8)), dma((2, 8)),
        dma((2,)), dma((2,)),
        dma((2, 2, 4)), dma((2, 2, 4)),
        dma((2,)), dma((2,)),
        dma((2, 4)), dma((2, 4)),
        dma((2, 8)), dma((2, 8)),
        dma((2, 8)), dma((2, 8)),
    ]
    return pl.pallas_call(
        kernel,
        out_shape=(
            jax.ShapeDtypeStruct(queries.shape, BF16),
            jax.ShapeDtypeStruct(key_weight.shape, F32),
            jax.ShapeDtypeStruct(value_weight.shape, F32),
        ),
        in_specs=[any_spec, any_spec, vmem, any_spec, any_spec, any_spec, any_spec],
        out_specs=(any_spec, vmem, vmem),
        scratch_shapes=scratch,
        compiler_params=pltpu.CompilerParams(
            collective_id=0, has_side_effects=True, vmem_limit_bytes=52 * 2**20
        ),
        cost_estimate=pl.CostEstimate(flops=4 * 10**9, bytes_accessed=10**7, transcendentals=655360),
    )(enc_terms, enc_resid, norm_gain.reshape(1, -1), key_weight, value_weight, queries, out_grad)


def solution(mesh):
    in_specs = (
        P("clip", "seq", None, None),
        P("clip", None, None),
        P(),
        P("clip", "seq"),
        P("clip", "seq"),
        P("clip", "seq", None),
        P("clip", "seq", None),
    )
    out_specs = (P("clip", "seq", None), P("clip", "seq"), P("clip", "seq"))
    return jax.shard_map(
        on_device, mesh=mesh, in_specs=in_specs, out_specs=out_specs, check_vma=False
    )
```

```python
import jax
import jax.numpy as jnp
from jax import lax
from jax.experimental import pallas as pl
from jax.experimental.pallas import tpu as pltpu
from jax.sharding import PartitionSpec as P

MESH = pl.DeviceIdType.MESH
HEAD = 128
F32 = jnp.float32
BF16 = jnp.bfloat16
CUTS = ((0, 128), (128, 384), (384, 640))


def dot(a, b, ca, cb):
    return lax.dot_general(a, b, (((ca,), (cb,)), ((), ())), preferred_element_type=F32)


def each(start, stop, body):
    lax.fori_loop(start, stop, lambda i, c: (body(i), c)[1], 0)


def device(x, z, k, l, y):
    return ((x * 4 + z) * 2 + k, l * 4 + y)


def kernel(
    enc, resid, gain, key_w, val_w, queries, grads,
    out_q, out_k, out_v,
    enc_buf, res_buf, ez_own, ez_recv, text32, text, text_t, w_own, w_all, kv_part, kv_recv, kv, q_buf, g_buf, qg_buf,
    pg_send, pg_own, pg_recv, gr_own, gr_all, dw_part, dw_recv, dw_mid,
    loc, e_s, e_r, ez_s, ez_r, t1_s, t1_r, t2_s, t2_r, t3_s, t3_r, w_s, w_r, wf_s, wf_r, kv_s, kv_r, kx_s, kx_r,
    qg_s, qg_r, px_s, px_r, oq_s, oq_r, ga_s, ga_r, dw_s, dw_r, dp_s, dp_r,
):
    clip, seq = lax.axis_index("clip"), lax.axis_index("seq")
    x, z, k = lax.div(clip, 8), lax.rem(lax.div(clip, 2), 4), lax.rem(clip, 2)
    l, y = lax.div(seq, 4), lax.rem(seq, 4)
    el, ek = 1 - l, 1 - k
    my_row, my_clip = z * 2 + k, k * 4 + x

    def y_dev(y2):
        return device(x, z, k, l, y2)

    def row_dev(e):
        return device(x, lax.div(e, 2), lax.rem(e, 2), l, y)

    def clip_dev(e):
        return device(lax.rem(e, 4), z, lax.div(e, 4), l, y)

    def others(n, me, body):
        each(1, n, lambda o: body(lax.rem(me + o, n)))

    def remote(src, dst, s, r, where):
        return pltpu.make_async_remote_copy(
            src_ref=src, dst_ref=dst, send_sem=s, recv_sem=r, device_id=where, device_id_type=MESH
        )

    def local(src, dst, i):
        return pltpu.make_async_copy(src, dst, loc.at[i])

    sends, arrivals = [], {}

    def arrive(name):
        for wait in arrivals.pop(name):
            wait()

    def flush():
        for name in list(arrivals):
            arrive(name)
        for wait in sends:
            wait()

    def group(name, n, me, copy):
        others(n, me, lambda e: copy(e, me).start())
        sends.append(lambda: others(n, me, lambda e: copy(e, me).wait_send()))
        arrivals[name] = [lambda: others(n, me, lambda e: copy(e, e).wait_recv())]

    def pair(name, copy, back):
        copy.start()
        sends.append(copy.wait_send)
        arrivals[name] = [back.wait_recv]

    def keep(name, copy):
        copy.start()
        arrivals.setdefault(name, []).append(copy.wait)

    def rows_of(i, n):
        return pl.ds(pl.multiple_of(i * n, n), n)

    def columns(j):
        return pl.ds(pl.multiple_of(j * 640, 128), 640)

    keep("enc", local(enc.at[0, 0, rows_of(y, 32)], enc_buf.at[y], 0))
    keep("resid", local(resid.at[0, rows_of(y, 32)], res_buf, 1))
    keep("w_own", local(key_w, w_own.at[0], 2))
    keep("w_own", local(val_w, w_own.at[1], 3))

    def qg_copy(i, l2, c, y2, slot):
        src, dst = ((queries, q_buf), (grads, g_buf))[i]
        lo, hi = CUTS[c]
        return remote(
            src.at[0, :, pl.ds(pl.multiple_of((l2 * 4 + y2) * 640 + lo, 128), hi - lo)],
            dst.at[l2, rows_of(slot, 128), pl.ds(lo, hi - lo)],
            qg_s.at[i, l2, c, y2], qg_r.at[i, l2, c, slot], y_dev(y2),
        )

    def qg_own(i, l2):
        src, dst = ((queries, q_buf), (grads, g_buf))[i]
        return local(src.at[0, :, columns(l2 * 4 + y)], dst.at[l2, rows_of(y, 128)], 4 + 2 * i + l2)

    def qg_start(name, l2, c):
        for i in range(2):
            group(f"{name}_{c}_{i}", 4, y, lambda y2, slot, i=i: qg_copy(i, l2, c, y2, slot))

    for i in range(2):
        keep("mine", qg_own(i, 0))
        keep("mine", qg_own(i, 1))

    bar = pltpu.get_barrier_semaphore()

    def greet(where):
        pl.semaphore_signal(bar, inc=1, device_id=where, device_id_type=MESH)

    others(4, y, lambda e: greet(y_dev(e)))
    greet(device(x, z, k, el, y))
    for o in (1, 3):
        for k2 in range(2):
            greet(device(x, lax.rem(z + o, 4), k2, l, y))
    greet(device(x, z, ek, l, y))
    others(8, my_clip, lambda e: greet(clip_dev(e)))
    pl.semaphore_wait(bar, 16)

    def enc_copy(h, y2, slot):
        cols = pl.ds(h * 2048, 2048)
        return remote(
            enc.at[0, 0, rows_of(y2, 32), cols], enc_buf.at[slot, :, cols], e_s.at[h, y2], e_r.at[h, slot], y_dev(y2)
        )

    group("enc_0", 4, y, lambda y2, slot: enc_copy(0, y2, slot))
    group("enc_1", 4, y, lambda y2, slot: enc_copy(1, y2, slot))

    arrive("w_own")

    def w_copy(e, slot):
        return remote(
            w_own.at[lax.rem(e, 2)], w_all.at[slot], w_s.at[e], w_r.at[slot], row_dev(e)
        )

    near = [(o, k2) for o in (1, 3) for k2 in range(2)]

    def near_row(o, k2):
        return lax.rem(z + o, 4) * 2 + k2

    def w_start(e):
        w_copy(e, my_row).start()
        sends.append(lambda: w_copy(e, my_row).wait_send())

    for o, k2 in near:
        w_start(near_row(o, k2))
    w_start(z * 2 + ek)
    arrivals["w_near"] = [lambda e=near_row(o, k2): w_copy(e, e).wait_recv() for o, k2 in near]
    arrivals["w"] = [lambda: w_copy(z * 2 + ek, z * 2 + ek).wait_recv()]
    keep("w", local(w_own.at[k], w_all.at[my_row], 8))

    arrive("enc")
    arrive("resid")
    for h in range(2):
        arrive(f"enc_{h}")
        for b in (2 * h, 2 * h + 1):
            cols = pl.ds(b * 1024, 1024)
            part = enc_buf[0, :, cols].astype(F32)
            for i in range(1, 4):
                part = part + enc_buf[i, :, cols].astype(F32)
            ez_own[:, cols] = part.astype(BF16)
        cols = pl.ds(h * 2048, 2048)
        ez = remote(ez_own.at[:, cols], ez_recv.at[:, cols], ez_s.at[h], ez_r.at[h], device(x, z, k, el, y))
        pair(f"ez_{h}", ez, ez)
    qg_start("own", l, 0)
    qg_start("far", el, 0)
    qg_start("own", l, 1)
    arrive("ez_0")
    arrive("ez_1")

    def hidden(b):
        cols = pl.ds(b * 1024, 1024)
        return (ez_own[:, cols].astype(F32) + ez_recv[:, cols].astype(F32)) + res_buf[:, cols].astype(F32)

    total = jnp.zeros((32, 1), F32)
    for b in range(4):
        h = hidden(b)
        total = total + jnp.sum(h * h, axis=1, keepdims=True)
    inv = lax.rsqrt(total * (1.0 / 4096.0) + 1e-06)
    for b in range(4):
        text32[b] = (hidden(b) * inv * gain[:, pl.ds(b * 1024, 1024)]).astype(BF16)

    def t1_copy(x2, slot):
        return remote(
            text32.at[x2], text.at[k, slot, rows_of(y, 32)], t1_s.at[x2], t1_r.at[slot], device(x2, z, k, l, y)
        )

    group("t1", 4, x, t1_copy)
    arrivals.pop("t1")
    keep("t1", local(text32.at[x], text.at[k, x, rows_of(y, 32)], 9))

    arrive("w_near")

    def w_pass(i):
        o = (3, 1)[i]
        part = w_all.at[pl.ds(lax.rem(z + o, 4) * 2, 2), pl.ds(64 * i, 64)]
        return remote(part, part, wf_s.at[i], wf_r.at[i], device(x, lax.rem(z + 4 - o, 4), k, l, y))

    def w_passed(i):
        part = w_all.at[pl.ds(lax.rem(z + 2, 4) * 2, 2), pl.ds(64 * i, 64)]
        return remote(part, part, wf_s.at[i], wf_r.at[i], device(x, lax.rem(z + 1, 4), k, l, y))

    for i in range(2):
        pair(f"w_far{i}", w_pass(i), w_passed(i))

    def t2_copy(x2, y2, slot):
        part = text.at[k, x2, rows_of(slot, 32)]
        return remote(part, part, t2_s.at[x2, y2], t2_r.at[x2, slot], y_dev(y2))

    order = (0, 2, 1, 3)
    for o in order:
        x2 = lax.rem(x + o, 4)
        if o == 0:
            arrive("t1")
        else:
            t1_copy(x2, x2).wait_recv()
        group(f"t2_{o}", 4, y, lambda y2, slot, x2=x2: t2_copy(x2, y2, slot))
    qg_start("far", el, 1)
    qg_start("own", l, 2)
    qg_start("far", el, 2)

    def t3_copy(core, x2):
        part = text.at[core, x2]
        return remote(part, part, t3_s.at[x2], t3_r.at[x2], device(x, z, ek, l, y))

    def kv_copy(e, slot):
        return remote(
            kv_part.at[lax.div(e, 4), lax.rem(e, 4)], kv_recv.at[lax.div(slot, 4), lax.rem(slot, 4)],
            kv_s.at[e], kv_r.at[slot], clip_dev(e),
        )

    def project(x2):
        t = text[:, x2].reshape(256, 1024)
        for lo, hi in ((0, 256), (256, 640)):
            acc = dot(t, w_all[:, :, lo:hi].reshape(1024, hi - lo), 1, 0)
            kv_part[:, x2, :, lo:hi] = acc.astype(BF16).reshape(2, 128, hi - lo)

    def kv_start(core, x2):
        e = core * 4 + x2
        kv_copy(e, my_clip).start()
        sends.append(lambda: kv_copy(e, my_clip).wait_send())

    for o in order:
        x2 = lax.rem(x + o, 4)
        arrive(f"t2_{o}")
        pair(f"t3_{o}", t3_copy(k, x2), t3_copy(ek, x2))
        if o == 0:
            arrive("w")
            arrive("w_far0")
            arrive("w_far1")
        arrive(f"t3_{o}")
        project(x2)
        if o == 0:
            keep("kv", local(kv_part.at[k, x], kv_recv.at[k, x], 10))
        else:
            kv_start(k, x2)
        kv_start(ek, x2)
    arrivals["kv"].append(lambda: others(8, my_clip, lambda e: kv_copy(e, e).wait_recv()))

    def turn(z2):
        text_t[z2] = text[:, :, :, rows_of(z2, 256)].reshape(1024, 256).T

    each(0, 4, turn)

    def kx_copy(c, slot):
        part = kv.at[slot, :, :, pl.ds(CUTS[c][0], CUTS[c][1] - CUTS[c][0])]
        return remote(part, part, kx_s.at[c], kx_r.at[c], device(x, z, k, el, y))

    def gather_kv(c):
        lo, hi = CUTS[c]
        for i in range(2):
            acc = kv_recv[i, 0, :, lo:hi].astype(F32)
            for b in range(1, 4):
                acc = acc + kv_recv[i, b, :, lo:hi].astype(F32)
            kv[l, i, :, lo:hi] = acc.astype(BF16)
        pair(f"kx{c}", kx_copy(c, l), kx_copy(c, el))

    scale = HEAD ** (-0.5)

    def head(l2, c, keep):
        cols = pl.ds(pl.multiple_of(c * HEAD, HEAD), HEAD)
        qh, gh = q_buf[l2, :, cols], g_buf[l2, :, cols]
        kh, vh = kv[l2, 0, :, cols], kv[l2, 1, :, cols]
        e = jnp.exp(dot(kh, qh, 1, 1) * scale)
        probs = e * (1.0 / jnp.sum(e, axis=0, keepdims=True))
        probs_b = probs.astype(BF16)
        dprobs = dot(vh, gh, 1, 1)
        delta = jnp.sum(probs_b.astype(F32) * dprobs, axis=0, keepdims=True)
        ds = (probs * (dprobs - delta)).astype(BF16)
        qg_buf[l2, :, cols] = (dot(ds, kh, 0, 0) * scale).astype(BF16)
        keep[0, :, cols] = (dot(ds, qh, 1, 0) * scale).astype(keep.dtype)
        keep[1, :, cols] = dot(probs_b, gh, 1, 0).astype(keep.dtype)

    def heads(l2, c, keep):
        lo, hi = CUTS[c]
        each(lo // HEAD, hi // HEAD, lambda h: head(l2, h, keep))

    def px_start(c):
        lo, hi = CUTS[c]
        cols = pl.ds(lo, hi - lo)
        copy = remote(
            pg_send.at[:, :, cols], pg_recv.at[:, :, cols], px_s.at[c], px_r.at[c], device(x, z, k, el, y)
        )
        pair(f"px{c}", copy, copy)

    def oq_copy(l2, y2, slot):
        return remote(
            qg_buf.at[l2, rows_of(y2, 128)], out_q.at[0, :, columns(l2 * 4 + slot)],
            oq_s.at[l2, y2], oq_r.at[l2, slot], y_dev(y2),
        )

    def oq_start(name, l2, i):
        group(name, 4, y, lambda y2, slot: oq_copy(l2, y2, slot))
        keep(name, local(qg_buf.at[l2, rows_of(y, 128)], out_q.at[0, :, columns(l2 * 4 + y)], i))

    def ga_copy(c, e, slot):
        cols = pl.ds(CUTS[c][0], CUTS[c][1] - CUTS[c][0])
        return remote(
            gr_own.at[lax.div(e, 4), :, cols], gr_all.at[lax.div(slot, 4), lax.rem(slot, 4), :, cols],
            ga_s.at[c, e], ga_r.at[c, slot], clip_dev(e),
        )

    def ga_start(c):
        lo, hi = CUTS[c]
        cols = pl.ds(lo, hi - lo)
        arrive(f"px{c}")
        gr_own[:, :, lo:hi] = (pg_own[:, :, lo:hi] + pg_recv[:, :, lo:hi].astype(F32)).astype(BF16)
        group(f"ga{c}", 8, my_clip, lambda e, slot: ga_copy(c, e, slot))
        keep(f"ga{c}", local(gr_own.at[k, :, cols], gr_all.at[k, x, :, cols], 19 + c))

    def dw_copy(c, e, slot):
        cols = pl.ds(CUTS[c][0], CUTS[c][1] - CUTS[c][0])
        return remote(
            dw_part.at[e, :, cols], dw_recv.at[lax.rem(slot, 2), lax.div(slot, 2), :, cols],
            dw_s.at[c, e], dw_r.at[c, slot], row_dev(e),
        )

    def dw_send(c, e):
        dw_copy(c, e, my_row).start()
        sends.append(lambda: dw_copy(c, e, my_row).wait_send())

    def dw_pass(c, i):
        cols = pl.ds(CUTS[c][0], CUTS[c][1] - CUTS[c][0])
        return remote(
            dw_part.at[lax.rem(z + 2, 4) * 2 + i, :, cols], dw_mid.at[i, :, cols],
            dp_s.at[c, i], dp_r.at[c, i], device(x, lax.rem(z + (1, 3)[i], 4), k, l, y),
        )

    def dw_start(c):
        lo, hi = CUTS[c]
        cols = pl.ds(lo, hi - lo)
        arrive(f"ga{c}")
        grads_c = gr_all[:, :, :, lo:hi].reshape(1024, hi - lo)

        def step(z2):
            acc = dot(text_t[z2], grads_c, 1, 0)
            dw_part[pl.ds(z2 * 2, 2), :, lo:hi] = acc.astype(BF16).reshape(2, 128, hi - lo)

        step(lax.rem(z + 2, 4))
        for i in range(2):
            pair(f"dp{c}{i}", dw_pass(c, i), dw_pass(c, i))
        for i, o in ((0, 1), (1, 3)):
            step(lax.rem(z + o, 4))
            dw_send(c, near_row(o, 1 - i))
        step(z)
        dw_send(c, z * 2 + ek)
        keep(f"dw{c}", local(dw_part.at[my_row, :, cols], dw_recv.at[k, z, :, cols], 22 + c))
        arrivals[f"dw{c}"] += [
            lambda e=e: dw_copy(c, e, e).wait_recv()
            for e in [near_row(o, k2) for o, k2 in near] + [z * 2 + ek]
        ]

    def dw_add(c):
        lo, hi = CUTS[c]
        for i, o in ((0, 1), (1, 3)):
            arrive(f"dp{c}{i}")
            e = near_row(o, i)
            both = dw_part[e, :, lo:hi].astype(F32) + dw_mid[i, :, lo:hi].astype(F32)
            dw_part[e, :, lo:hi] = both.astype(BF16)
            dw_send(c, e)

    def dw_end(c):
        lo, hi = CUTS[c]
        arrive(f"dw{c}")
        for i, out in ((0, out_k), (1, out_v)):
            acc = dw_recv[i, z, :, lo:hi].astype(F32)
            for o in (1, 3):
                acc = acc + dw_recv[i, lax.rem(z + o, 4), :, lo:hi].astype(F32)
            out[:, lo:hi] = acc

    last = len(CUTS) - 1
    arrive("kv")
    gather_kv(0)
    arrive("mine")

    def heads_of(name, l2, c, kept):
        for i in range(2):
            arrive(f"{name}_{c}_{i}")
        heads(l2, c, kept)

    heads_of("own", l, 0, pg_own)
    for c in range(len(CUTS)):
        if c < last:
            gather_kv(c + 1)
        if c == 0:
            pass
        arrive(f"kx{c}")
        heads_of("far", el, c, pg_send)
        px_start(c)
        if c < last:
            heads_of("own", l, c + 1, pg_own)
        if c == max(0, last - 1):
            oq_start("oq_own", l, 12)
        if c == last:
            oq_start("oq_far", el, 13)
        if c > 0:
            dw_start(c - 1)
        ga_start(c)
        if c > 0:
            dw_add(c - 1)
    dw_start(last)
    dw_add(last)
    for c in range(len(CUTS)):
        dw_end(c)
    flush()


def on_device(enc_terms, enc_resid, norm_gain, key_weight, value_weight, queries, out_grad):
    any_spec = pl.BlockSpec(memory_space=pl.ANY)
    vmem = pl.BlockSpec(memory_space=pltpu.VMEM)
    dma = pltpu.SemaphoreType.DMA
    scratch = [
        pltpu.VMEM((4, 32, 4096), BF16),
        pltpu.VMEM((32, 4096), BF16),
        pltpu.VMEM((32, 4096), BF16),
        pltpu.VMEM((32, 4096), BF16),
        pltpu.VMEM((4, 32, 1024), BF16),
        pltpu.VMEM((2, 4, 128, 1024), BF16),
        pltpu.VMEM((4, 256, 1024), BF16),
        pltpu.VMEM((2, 128, 640), BF16),
        pltpu.VMEM((8, 128, 640), BF16),
        pltpu.VMEM((2, 4, 128, 640), BF16),
        pltpu.VMEM((2, 4, 128, 640), BF16),
        pltpu.VMEM((2, 2, 128, 640), BF16),
        pltpu.VMEM((2, 512, 640), BF16),
        pltpu.VMEM((2, 512, 640), BF16),
        pltpu.VMEM((2, 512, 640), BF16),
        pltpu.VMEM((2, 128, 640), BF16),
        pltpu.VMEM((2, 128, 640), F32),
        pltpu.VMEM((2, 128, 640), BF16),
        pltpu.VMEM((2, 128, 640), BF16),
        pltpu.VMEM((2, 4, 128, 640), BF16),
        pltpu.VMEM((8, 128, 640), BF16),
        pltpu.VMEM((2, 4, 128, 640), BF16),
        pltpu.VMEM((2, 128, 640), BF16),
        dma((25,)),
        dma((2, 4)), dma((2, 4)),
        dma((2,)), dma((2,)),
        dma((4,)), dma((4,)),
        dma((4, 4)), dma((4, 4)),
        dma((4,)), dma((4,)),
        dma((8,)), dma((8,)),
        dma((2,)), dma((2,)),
        dma((8,)), dma((8,)),
        dma((3,)), dma((3,)),
        dma((2, 2, 3, 4)), dma((2, 2, 3, 4)),
        dma((3,)), dma((3,)),
        dma((2, 4)), dma((2, 4)),
        dma((3, 8)), dma((3, 8)),
        dma((3, 8)), dma((3, 8)),
        dma((3, 2)), dma((3, 2)),
    ]
    return pl.pallas_call(
        kernel,
        out_shape=(
            jax.ShapeDtypeStruct(queries.shape, BF16),
            jax.ShapeDtypeStruct(key_weight.shape, F32),
            jax.ShapeDtypeStruct(value_weight.shape, F32),
        ),
        in_specs=[any_spec, any_spec, vmem, any_spec, any_spec, any_spec, any_spec],
        out_specs=(any_spec, vmem, vmem),
        scratch_shapes=scratch,
        compiler_params=pltpu.CompilerParams(
            collective_id=0, has_side_effects=True, vmem_limit_bytes=62 * 2**20
        ),
        cost_estimate=pl.CostEstimate(flops=4 * 10**9, bytes_accessed=10**7, transcendentals=655360),
    )(enc_terms, enc_resid, norm_gain.reshape(1, -1), key_weight, value_weight, queries, out_grad)


def solution(mesh):
    in_specs = (
        P("clip", "seq", None, None),
        P("clip", None, None),
        P(),
        P("clip", "seq"),
        P("clip", "seq"),
        P("clip", "seq", None),
        P("clip", "seq", None),
    )
    out_specs = (P("clip", "seq", None), P("clip", "seq"), P("clip", "seq"))
    return jax.shard_map(
        on_device, mesh=mesh, in_specs=in_specs, out_specs=out_specs, check_vma=False
    )
```

```python
import jax
import jax.numpy as jnp
from jax import lax
from jax.experimental import pallas as pl
from jax.experimental.pallas import tpu as pltpu
from jax.sharding import PartitionSpec as P

MESH = pl.DeviceIdType.MESH
HEAD = 128
F32 = jnp.float32
BF16 = jnp.bfloat16
CUTS = ((0, 128), (128, 384), (384, 640))
EARLY = 2
HOLD = 0


def dot(a, b, ca, cb):
    return lax.dot_general(a, b, (((ca,), (cb,)), ((), ())), preferred_element_type=F32)


def each(start, stop, body):
    lax.fori_loop(start, stop, lambda i, c: (body(i), c)[1], 0)


def device(x, z, k, l, y):
    return ((x * 4 + z) * 2 + k, l * 4 + y)


def kernel(
    enc, resid, gain, key_w, val_w, queries, grads,
    out_q, out_k, out_v,
    enc_buf, res_buf, ez_own, ez_recv, text32, text, text_t, w_own, w_all, kv_part, kv_recv, kv, q_buf, g_buf, qg_buf,
    pg_send, pg_own, pg_recv, gr_own, gr_all, dw_part, dw_recv, dw_mid,
    loc, e_s, e_r, ez_s, ez_r, t1_s, t1_r, t2_s, t2_r, t3_s, t3_r, w_s, w_r, wf_s, wf_r, kv_s, kv_r, kx_s, kx_r,
    qg_s, qg_r, px_s, px_r, oq_s, oq_r, ga_s, ga_r, dw_s, dw_r, dp_s, dp_r,
):
    clip, seq = lax.axis_index("clip"), lax.axis_index("seq")
    x, z, k = lax.div(clip, 8), lax.rem(lax.div(clip, 2), 4), lax.rem(clip, 2)
    l, y = lax.div(seq, 4), lax.rem(seq, 4)
    el, ek = 1 - l, 1 - k
    my_row, my_clip = z * 2 + k, k * 4 + x

    def y_dev(y2):
        return device(x, z, k, l, y2)

    def row_dev(e):
        return device(x, lax.div(e, 2), lax.rem(e, 2), l, y)

    def clip_dev(e):
        return device(lax.rem(e, 4), z, lax.div(e, 4), l, y)

    def others(n, me, body):
        each(1, n, lambda o: body(lax.rem(me + o, n)))

    def remote(src, dst, s, r, where):
        return pltpu.make_async_remote_copy(
            src_ref=src, dst_ref=dst, send_sem=s, recv_sem=r, device_id=where, device_id_type=MESH
        )

    def local(src, dst, i):
        return pltpu.make_async_copy(src, dst, loc.at[i])

    sends, arrivals = [], {}

    def arrive(name):
        for wait in arrivals.pop(name):
            wait()

    def flush():
        for name in list(arrivals):
            arrive(name)
        for wait in sends:
            wait()

    def group(name, n, me, copy):
        others(n, me, lambda e: copy(e, me).start())
        sends.append(lambda: others(n, me, lambda e: copy(e, me).wait_send()))
        arrivals[name] = [lambda: others(n, me, lambda e: copy(e, e).wait_recv())]

    def pair(name, copy, back):
        copy.start()
        sends.append(copy.wait_send)
        arrivals[name] = [back.wait_recv]

    def keep(name, copy):
        copy.start()
        arrivals.setdefault(name, []).append(copy.wait)

    def rows_of(i, n):
        return pl.ds(pl.multiple_of(i * n, n), n)

    def columns(j):
        return pl.ds(pl.multiple_of(j * 640, 128), 640)

    keep("enc", local(enc.at[0, 0, rows_of(y, 32)], enc_buf.at[y], 0))
    keep("resid", local(resid.at[0, rows_of(y, 32)], res_buf, 1))
    keep("w_own", local(key_w, w_own.at[0], 2))
    keep("w_own", local(val_w, w_own.at[1], 3))

    def qg_copy(i, l2, c, y2, slot):
        src, dst = ((queries, q_buf), (grads, g_buf))[i]
        lo, hi = CUTS[c]
        return remote(
            src.at[0, :, pl.ds(pl.multiple_of((l2 * 4 + y2) * 640 + lo, 128), hi - lo)],
            dst.at[l2, rows_of(slot, 128), pl.ds(lo, hi - lo)],
            qg_s.at[i, l2, c, y2], qg_r.at[i, l2, c, slot], y_dev(y2),
        )

    def qg_own(i, l2):
        src, dst = ((queries, q_buf), (grads, g_buf))[i]
        return local(src.at[0, :, columns(l2 * 4 + y)], dst.at[l2, rows_of(y, 128)], 4 + 2 * i + l2)

    def qg_start(name, l2, c):
        for i in range(2):
            group(f"{name}_{c}_{i}", 4, y, lambda y2, slot, i=i: qg_copy(i, l2, c, y2, slot))

    pieces = [p for c in range(len(CUTS)) for p in (("own", l, c), ("far", el, c))]
    early, late = pieces[:EARLY], pieces[EARLY:]
    for i in range(2):
        keep("mine", qg_own(i, 0))
        keep("mine", qg_own(i, 1))

    bar = pltpu.get_barrier_semaphore()

    def greet(where):
        pl.semaphore_signal(bar, inc=1, device_id=where, device_id_type=MESH)

    others(4, y, lambda e: greet(y_dev(e)))
    greet(device(x, z, k, el, y))
    for o in (1, 3):
        for k2 in range(2):
            greet(device(x, lax.rem(z + o, 4), k2, l, y))
    greet(device(x, z, ek, l, y))
    others(8, my_clip, lambda e: greet(clip_dev(e)))
    pl.semaphore_wait(bar, 16)

    def enc_copy(h, y2, slot):
        cols = pl.ds(h * 2048, 2048)
        return remote(
            enc.at[0, 0, rows_of(y2, 32), cols], enc_buf.at[slot, :, cols], e_s.at[h, y2], e_r.at[h, slot], y_dev(y2)
        )

    group("enc_0", 4, y, lambda y2, slot: enc_copy(0, y2, slot))
    group("enc_1", 4, y, lambda y2, slot: enc_copy(1, y2, slot))

    arrive("w_own")

    def w_copy(e, slot):
        return remote(
            w_own.at[lax.rem(e, 2)], w_all.at[slot], w_s.at[e], w_r.at[slot], row_dev(e)
        )

    near = [(o, k2) for o in (1, 3) for k2 in range(2)]

    def near_row(o, k2):
        return lax.rem(z + o, 4) * 2 + k2

    def w_start(e):
        w_copy(e, my_row).start()
        sends.append(lambda: w_copy(e, my_row).wait_send())

    for o, k2 in near:
        w_start(near_row(o, k2))
    w_start(z * 2 + ek)
    arrivals["w_near"] = [lambda e=near_row(o, k2): w_copy(e, e).wait_recv() for o, k2 in near]
    arrivals["w"] = [lambda: w_copy(z * 2 + ek, z * 2 + ek).wait_recv()]
    keep("w", local(w_own.at[k], w_all.at[my_row], 8))

    arrive("enc")
    arrive("resid")
    for h in range(2):
        arrive(f"enc_{h}")
        for b in (2 * h, 2 * h + 1):
            cols = pl.ds(b * 1024, 1024)
            part = enc_buf[0, :, cols].astype(F32)
            for i in range(1, 4):
                part = part + enc_buf[i, :, cols].astype(F32)
            ez_own[:, cols] = part.astype(BF16)
        cols = pl.ds(h * 2048, 2048)
        ez = remote(ez_own.at[:, cols], ez_recv.at[:, cols], ez_s.at[h], ez_r.at[h], device(x, z, k, el, y))
        pair(f"ez_{h}", ez, ez)
    for name, l2, c in early:
        qg_start(name, l2, c)
    arrive("ez_0")
    arrive("ez_1")

    def hidden(b):
        cols = pl.ds(b * 1024, 1024)
        return (ez_own[:, cols].astype(F32) + ez_recv[:, cols].astype(F32)) + res_buf[:, cols].astype(F32)

    total = jnp.zeros((32, 1), F32)
    for b in range(4):
        h = hidden(b)
        total = total + jnp.sum(h * h, axis=1, keepdims=True)
    inv = lax.rsqrt(total * (1.0 / 4096.0) + 1e-06)
    for b in range(4):
        text32[b] = (hidden(b) * inv * gain[:, pl.ds(b * 1024, 1024)]).astype(BF16)

    def t1_copy(x2, slot):
        return remote(
            text32.at[x2], text.at[k, slot, rows_of(y, 32)], t1_s.at[x2], t1_r.at[slot], device(x2, z, k, l, y)
        )

    group("t1", 4, x, t1_copy)
    arrivals.pop("t1")
    keep("t1", local(text32.at[x], text.at[k, x, rows_of(y, 32)], 9))

    arrive("w_near")

    def w_pass(i):
        o = (3, 1)[i]
        part = w_all.at[pl.ds(lax.rem(z + o, 4) * 2, 2), pl.ds(64 * i, 64)]
        return remote(part, part, wf_s.at[i], wf_r.at[i], device(x, lax.rem(z + 4 - o, 4), k, l, y))

    def w_passed(i):
        part = w_all.at[pl.ds(lax.rem(z + 2, 4) * 2, 2), pl.ds(64 * i, 64)]
        return remote(part, part, wf_s.at[i], wf_r.at[i], device(x, lax.rem(z + 1, 4), k, l, y))

    for i in range(2):
        pair(f"w_far{i}", w_pass(i), w_passed(i))

    def t2_copy(x2, y2, slot):
        part = text.at[k, x2, rows_of(slot, 32)]
        return remote(part, part, t2_s.at[x2, y2], t2_r.at[x2, slot], y_dev(y2))

    order = (0, 2, 1, 3)
    for o in order:
        x2 = lax.rem(x + o, 4)
        if o == 0:
            arrive("t1")
        else:
            t1_copy(x2, x2).wait_recv()
        group(f"t2_{o}", 4, y, lambda y2, slot, x2=x2: t2_copy(x2, y2, slot))
    for name, l2, c in late:
        qg_start(name, l2, c)

    def t3_copy(core, x2):
        part = text.at[core, x2]
        return remote(part, part, t3_s.at[x2], t3_r.at[x2], device(x, z, ek, l, y))

    def kv_copy(c, e, slot):
        cols = pl.ds(CUTS[c][0], CUTS[c][1] - CUTS[c][0])
        return remote(
            kv_part.at[lax.div(e, 4), lax.rem(e, 4), :, cols],
            kv_recv.at[lax.div(slot, 4), lax.rem(slot, 4), :, cols],
            kv_s.at[c, e], kv_r.at[c, slot], clip_dev(e),
        )

    def project(x2):
        t = text[:, x2].reshape(256, 1024)
        for lo, hi in ((0, 256), (256, 640)):
            acc = dot(t, w_all[:, :, lo:hi].reshape(1024, hi - lo), 1, 0)
            kv_part[:, x2, :, lo:hi] = acc.astype(BF16).reshape(2, 128, hi - lo)

    def kv_start(c, core, x2):
        e = core * 4 + x2
        kv_copy(c, e, my_clip).start()
        sends.append(lambda: kv_copy(c, e, my_clip).wait_send())

    def kv_block(c, o):
        x2 = lax.rem(x + o, 4)
        cols = pl.ds(CUTS[c][0], CUTS[c][1] - CUTS[c][0])
        if o == 0:
            keep(f"kv{c}", local(kv_part.at[k, x, :, cols], kv_recv.at[k, x, :, cols], 14 + 2 * len(CUTS) + c))
        else:
            kv_start(c, k, x2)
        kv_start(c, ek, x2)

    held_parts = range(1, len(CUTS))
    held = []
    for o in order:
        x2 = lax.rem(x + o, 4)
        arrive(f"t2_{o}")
        pair(f"t3_{o}", t3_copy(k, x2), t3_copy(ek, x2))
        if o == 0:
            arrive("w")
            arrive("w_far0")
            arrive("w_far1")
        arrive(f"t3_{o}")
        project(x2)
        kv_block(0, o)
        for c in held_parts:
            held.append((c, o))
        if len(held) > HOLD * len(held_parts):
            for c, o2 in held[: len(held_parts)]:
                kv_block(c, o2)
            held = held[len(held_parts) :]
    for c, o2 in sorted(held):
        kv_block(c, o2)
    for c in range(len(CUTS)):
        arrivals[f"kv{c}"].append(lambda c=c: others(8, my_clip, lambda e: kv_copy(c, e, e).wait_recv()))

    def turn(z2):
        text_t[z2] = text[:, :, :, rows_of(z2, 256)].reshape(1024, 256).T

    each(0, 4, turn)

    def kx_copy(c, slot):
        part = kv.at[slot, :, :, pl.ds(CUTS[c][0], CUTS[c][1] - CUTS[c][0])]
        return remote(part, part, kx_s.at[c], kx_r.at[c], device(x, z, k, el, y))

    def gather_kv(c):
        lo, hi = CUTS[c]
        arrive(f"kv{c}")
        for i in range(2):
            acc = kv_recv[i, 0, :, lo:hi].astype(F32)
            for b in range(1, 4):
                acc = acc + kv_recv[i, b, :, lo:hi].astype(F32)
            kv[l, i, :, lo:hi] = acc.astype(BF16)
        pair(f"kx{c}", kx_copy(c, l), kx_copy(c, el))

    scale = HEAD ** (-0.5)

    def head(l2, c, keep):
        cols = pl.ds(pl.multiple_of(c * HEAD, HEAD), HEAD)
        qh, gh = q_buf[l2, :, cols], g_buf[l2, :, cols]
        kh, vh = kv[l2, 0, :, cols], kv[l2, 1, :, cols]
        e = jnp.exp(dot(kh, qh, 1, 1) * scale)
        probs = e * (1.0 / jnp.sum(e, axis=0, keepdims=True))
        probs_b = probs.astype(BF16)
        dprobs = dot(vh, gh, 1, 1)
        delta = jnp.sum(probs_b.astype(F32) * dprobs, axis=0, keepdims=True)
        ds = (probs * (dprobs - delta)).astype(BF16)
        qg_buf[l2, :, cols] = (dot(ds, kh, 0, 0) * scale).astype(BF16)
        keep[0, :, cols] = (dot(ds, qh, 1, 0) * scale).astype(keep.dtype)
        keep[1, :, cols] = dot(probs_b, gh, 1, 0).astype(keep.dtype)

    def heads(l2, c, keep):
        lo, hi = CUTS[c]
        each(lo // HEAD, hi // HEAD, lambda h: head(l2, h, keep))

    def px_start(c):
        lo, hi = CUTS[c]
        cols = pl.ds(lo, hi - lo)
        copy = remote(
            pg_send.at[:, :, cols], pg_recv.at[:, :, cols], px_s.at[c], px_r.at[c], device(x, z, k, el, y)
        )
        pair(f"px{c}", copy, copy)

    def oq_copy(l2, y2, slot):
        return remote(
            qg_buf.at[l2, rows_of(y2, 128)], out_q.at[0, :, columns(l2 * 4 + slot)],
            oq_s.at[l2, y2], oq_r.at[l2, slot], y_dev(y2),
        )

    def oq_start(name, l2, i):
        group(name, 4, y, lambda y2, slot: oq_copy(l2, y2, slot))
        keep(name, local(qg_buf.at[l2, rows_of(y, 128)], out_q.at[0, :, columns(l2 * 4 + y)], i))

    def ga_copy(c, e, slot):
        cols = pl.ds(CUTS[c][0], CUTS[c][1] - CUTS[c][0])
        return remote(
            gr_own.at[lax.div(e, 4), :, cols], gr_all.at[lax.div(slot, 4), lax.rem(slot, 4), :, cols],
            ga_s.at[c, e], ga_r.at[c, slot], clip_dev(e),
        )

    def ga_start(c):
        lo, hi = CUTS[c]
        cols = pl.ds(lo, hi - lo)
        arrive(f"px{c}")
        gr_own[:, :, lo:hi] = (pg_own[:, :, lo:hi] + pg_recv[:, :, lo:hi].astype(F32)).astype(BF16)
        group(f"ga{c}", 8, my_clip, lambda e, slot: ga_copy(c, e, slot))
        keep(f"ga{c}", local(gr_own.at[k, :, cols], gr_all.at[k, x, :, cols], 14 + c))

    def dw_copy(c, e, slot):
        cols = pl.ds(CUTS[c][0], CUTS[c][1] - CUTS[c][0])
        return remote(
            dw_part.at[e, :, cols], dw_recv.at[lax.rem(slot, 2), lax.div(slot, 2), :, cols],
            dw_s.at[c, e], dw_r.at[c, slot], row_dev(e),
        )

    def dw_send(c, e):
        dw_copy(c, e, my_row).start()
        sends.append(lambda: dw_copy(c, e, my_row).wait_send())

    def dw_pass(c, i):
        cols = pl.ds(CUTS[c][0], CUTS[c][1] - CUTS[c][0])
        return remote(
            dw_part.at[lax.rem(z + 2, 4) * 2 + i, :, cols], dw_mid.at[i, :, cols],
            dp_s.at[c, i], dp_r.at[c, i], device(x, lax.rem(z + (1, 3)[i], 4), k, l, y),
        )

    def dw_start(c):
        lo, hi = CUTS[c]
        cols = pl.ds(lo, hi - lo)
        arrive(f"ga{c}")
        grads_c = gr_all[:, :, :, lo:hi].reshape(1024, hi - lo)

        def step(z2):
            acc = dot(text_t[z2], grads_c, 1, 0)
            dw_part[pl.ds(z2 * 2, 2), :, lo:hi] = acc.astype(BF16).reshape(2, 128, hi - lo)

        step(lax.rem(z + 2, 4))
        for i in range(2):
            pair(f"dp{c}{i}", dw_pass(c, i), dw_pass(c, i))
        for i, o in ((0, 1), (1, 3)):
            step(lax.rem(z + o, 4))
            dw_send(c, near_row(o, 1 - i))
        step(z)
        dw_send(c, z * 2 + ek)
        keep(f"dw{c}", local(dw_part.at[my_row, :, cols], dw_recv.at[k, z, :, cols], 14 + len(CUTS) + c))
        arrivals[f"dw{c}"] += [
            lambda e=e: dw_copy(c, e, e).wait_recv()
            for e in [near_row(o, k2) for o, k2 in near] + [z * 2 + ek]
        ]

    def dw_add(c):
        lo, hi = CUTS[c]
        for i, o in ((0, 1), (1, 3)):
            arrive(f"dp{c}{i}")
            e = near_row(o, i)
            both = dw_part[e, :, lo:hi].astype(F32) + dw_mid[i, :, lo:hi].astype(F32)
            dw_part[e, :, lo:hi] = both.astype(BF16)
            dw_send(c, e)

    def dw_end(c):
        lo, hi = CUTS[c]
        arrive(f"dw{c}")
        for i, out in ((0, out_k), (1, out_v)):
            acc = dw_recv[i, z, :, lo:hi].astype(F32)
            for o in (1, 3):
                acc = acc + dw_recv[i, lax.rem(z + o, 4), :, lo:hi].astype(F32)
            out[:, lo:hi] = acc

    last = len(CUTS) - 1
    arrive("mine")

    def heads_of(name, l2, c, kept):
        for i in range(2):
            arrive(f"{name}_{c}_{i}")
        heads(l2, c, kept)

    for c in range(len(CUTS)):
        gather_kv(c)
        heads_of("own", l, c, pg_own)
        if c > 0:
            ga_start(c - 1)
        arrive(f"kx{c}")
        heads_of("far", el, c, pg_send)
        px_start(c)
        if c == last:
            oq_start("oq_own", l, 12)
            oq_start("oq_far", el, 13)
            if last > 0:
                dw_start(0)
            ga_start(c)
    for c in range(len(CUTS)):
        if c > 0 or last == 0:
            dw_start(c)
        if c > 0:
            dw_add(c - 1)
    dw_add(last)
    for c in range(len(CUTS)):
        dw_end(c)
    flush()


def on_device(enc_terms, enc_resid, norm_gain, key_weight, value_weight, queries, out_grad):
    any_spec = pl.BlockSpec(memory_space=pl.ANY)
    vmem = pl.BlockSpec(memory_space=pltpu.VMEM)
    dma = pltpu.SemaphoreType.DMA
    n = len(CUTS)
    scratch = [
        pltpu.VMEM((4, 32, 4096), BF16),
        pltpu.VMEM((32, 4096), BF16),
        pltpu.VMEM((32, 4096), BF16),
        pltpu.VMEM((32, 4096), BF16),
        pltpu.VMEM((4, 32, 1024), BF16),
        pltpu.VMEM((2, 4, 128, 1024), BF16),
        pltpu.VMEM((4, 256, 1024), BF16),
        pltpu.VMEM((2, 128, 640), BF16),
        pltpu.VMEM((8, 128, 640), BF16),
        pltpu.VMEM((2, 4, 128, 640), BF16),
        pltpu.VMEM((2, 4, 128, 640), BF16),
        pltpu.VMEM((2, 2, 128, 640), BF16),
        pltpu.VMEM((2, 512, 640), BF16),
        pltpu.VMEM((2, 512, 640), BF16),
        pltpu.VMEM((2, 512, 640), BF16),
        pltpu.VMEM((2, 128, 640), BF16),
        pltpu.VMEM((2, 128, 640), F32),
        pltpu.VMEM((2, 128, 640), BF16),
        pltpu.VMEM((2, 128, 640), BF16),
        pltpu.VMEM((2, 4, 128, 640), BF16),
        pltpu.VMEM((8, 128, 640), BF16),
        pltpu.VMEM((2, 4, 128, 640), BF16),
        pltpu.VMEM((2, 128, 640), BF16),
        dma((14 + 3 * n,)),
        dma((2, 4)), dma((2, 4)),
        dma((2,)), dma((2,)),
        dma((4,)), dma((4,)),
        dma((4, 4)), dma((4, 4)),
        dma((4,)), dma((4,)),
        dma((8,)), dma((8,)),
        dma((2,)), dma((2,)),
        dma((n, 8)), dma((n, 8)),
        dma((n,)), dma((n,)),
        dma((2, 2, n, 4)), dma((2, 2, n, 4)),
        dma((n,)), dma((n,)),
        dma((2, 4)), dma((2, 4)),
        dma((n, 8)), dma((n, 8)),
        dma((n, 8)), dma((n, 8)),
        dma((n, 2)), dma((n, 2)),
    ]
    return pl.pallas_call(
        kernel,
        out_shape=(
            jax.ShapeDtypeStruct(queries.shape, BF16),
            jax.ShapeDtypeStruct(key_weight.shape, F32),
            jax.ShapeDtypeStruct(value_weight.shape, F32),
        ),
        in_specs=[any_spec, any_spec, vmem, any_spec, any_spec, any_spec, any_spec],
        out_specs=(any_spec, vmem, vmem),
        scratch_shapes=scratch,
        compiler_params=pltpu.CompilerParams(
            collective_id=0, has_side_effects=True, vmem_limit_bytes=62 * 2**20
        ),
        cost_estimate=pl.CostEstimate(flops=4 * 10**9, bytes_accessed=10**7, transcendentals=655360),
    )(enc_terms, enc_resid, norm_gain.reshape(1, -1), key_weight, value_weight, queries, out_grad)


def solution(mesh):
    in_specs = (
        P("clip", "seq", None, None),
        P("clip", None, None),
        P(),
        P("clip", "seq"),
        P("clip", "seq"),
        P("clip", "seq", None),
        P("clip", "seq", None),
    )
    out_specs = (P("clip", "seq", None), P("clip", "seq"), P("clip", "seq"))
    return jax.shard_map(
        on_device, mesh=mesh, in_specs=in_specs, out_specs=out_specs, check_vma=False
    )
```

```python
import jax
import jax.numpy as jnp
from jax import lax
from jax.experimental import pallas as pl
from jax.experimental.pallas import tpu as pltpu
from jax.sharding import PartitionSpec as P

MESH = pl.DeviceIdType.MESH
HEAD = 128
F32 = jnp.float32
BF16 = jnp.bfloat16
CUTS = ((0, 128), (128, 384), (384, 640))
EARLY = 2
HOLD = 0


def dot(a, b, ca, cb):
    return lax.dot_general(a, b, (((ca,), (cb,)), ((), ())), preferred_element_type=F32)


def each(start, stop, body):
    lax.fori_loop(start, stop, lambda i, c: (body(i), c)[1], 0)


def device(x, z, k, l, y):
    return ((x * 4 + z) * 2 + k, l * 4 + y)


def kernel(
    enc, resid, gain, key_w, val_w, queries, grads,
    out_q, out_k, out_v,
    enc_buf, res_buf, ez_own, ez_recv, text32, text, text_t, w_own, w_all, kv_part, kv_recv, kv, q_buf, g_buf, qg_buf,
    pg_send, pg_own, pg_recv, gr_own, gr_all, dw_part, dw_recv, dw_mid,
    loc, e_s, e_r, ez_s, ez_r, t1_s, t1_r, t2_s, t2_r, t3_s, t3_r, w_s, w_r, wf_s, wf_r, kv_s, kv_r, kx_s, kx_r,
    qg_s, qg_r, px_s, px_r, oq_s, oq_r, ga_s, ga_r, dw_s, dw_r, dp_s, dp_r,
):
    clip, seq = lax.axis_index("clip"), lax.axis_index("seq")
    x, z, k = lax.div(clip, 8), lax.rem(lax.div(clip, 2), 4), lax.rem(clip, 2)
    l, y = lax.div(seq, 4), lax.rem(seq, 4)
    el, ek = 1 - l, 1 - k
    my_row, my_clip = z * 2 + k, k * 4 + x

    def y_dev(y2):
        return device(x, z, k, l, y2)

    def row_dev(e):
        return device(x, lax.div(e, 2), lax.rem(e, 2), l, y)

    def clip_dev(e):
        return device(lax.rem(e, 4), z, lax.div(e, 4), l, y)

    def others(n, me, body):
        each(1, n, lambda o: body(lax.rem(me + o, n)))

    def remote(src, dst, s, r, where):
        return pltpu.make_async_remote_copy(
            src_ref=src, dst_ref=dst, send_sem=s, recv_sem=r, device_id=where, device_id_type=MESH
        )

    def local(src, dst, i):
        return pltpu.make_async_copy(src, dst, loc.at[i])

    sends, arrivals = [], {}

    def arrive(name):
        for wait in arrivals.pop(name):
            wait()

    def flush():
        for name in list(arrivals):
            arrive(name)
        for wait in sends:
            wait()

    def group(name, n, me, copy):
        others(n, me, lambda e: copy(e, me).start())
        sends.append(lambda: others(n, me, lambda e: copy(e, me).wait_send()))
        arrivals[name] = [lambda: others(n, me, lambda e: copy(e, e).wait_recv())]

    def pair(name, copy, back):
        copy.start()
        sends.append(copy.wait_send)
        arrivals[name] = [back.wait_recv]

    def keep(name, copy):
        copy.start()
        arrivals.setdefault(name, []).append(copy.wait)

    def rows_of(i, n):
        return pl.ds(pl.multiple_of(i * n, n), n)

    def columns(j):
        return pl.ds(pl.multiple_of(j * 640, 128), 640)

    keep("enc", local(enc.at[0, 0, rows_of(y, 32)], enc_buf.at[y], 0))
    keep("resid", local(resid.at[0, rows_of(y, 32)], res_buf, 1))
    keep("w_own", local(key_w, w_own.at[0], 2))
    keep("w_own", local(val_w, w_own.at[1], 3))

    def qg_copy(i, l2, c, y2, slot):
        src, dst = ((queries, q_buf), (grads, g_buf))[i]
        lo, hi = CUTS[c]
        return remote(
            src.at[0, :, pl.ds(pl.multiple_of((l2 * 4 + y2) * 640 + lo, 128), hi - lo)],
            dst.at[l2, rows_of(slot, 128), pl.ds(lo, hi - lo)],
            qg_s.at[i, l2, c, y2], qg_r.at[i, l2, c, slot], y_dev(y2),
        )

    def qg_own(i, l2):
        src, dst = ((queries, q_buf), (grads, g_buf))[i]
        return local(src.at[0, :, columns(l2 * 4 + y)], dst.at[l2, rows_of(y, 128)], 4 + 2 * i + l2)

    def qg_start(name, l2, c):
        for i in range(2):
            group(f"{name}_{c}_{i}", 4, y, lambda y2, slot, i=i: qg_copy(i, l2, c, y2, slot))

    pieces = [p for c in range(len(CUTS)) for p in (("own", l, c), ("far", el, c))]
    early, late = pieces[:EARLY], pieces[EARLY:]
    for i in range(2):
        keep("mine", qg_own(i, 0))
        keep("mine", qg_own(i, 1))

    bar = pltpu.get_barrier_semaphore()

    def greet(where):
        pl.semaphore_signal(bar, inc=1, device_id=where, device_id_type=MESH)

    others(4, y, lambda e: greet(y_dev(e)))
    greet(device(x, z, k, el, y))
    for o in (1, 3):
        for k2 in range(2):
            greet(device(x, lax.rem(z + o, 4), k2, l, y))
    greet(device(x, z, ek, l, y))
    others(8, my_clip, lambda e: greet(clip_dev(e)))
    pl.semaphore_wait(bar, 16)

    def enc_copy(h, y2, slot):
        cols = pl.ds(h * 2048, 2048)
        return remote(
            enc.at[0, 0, rows_of(y2, 32), cols], enc_buf.at[slot, :, cols], e_s.at[h, y2], e_r.at[h, slot], y_dev(y2)
        )

    group("enc_0", 4, y, lambda y2, slot: enc_copy(0, y2, slot))
    group("enc_1", 4, y, lambda y2, slot: enc_copy(1, y2, slot))

    arrive("w_own")

    def w_copy(e, slot):
        return remote(
            w_own.at[lax.rem(e, 2)], w_all.at[slot], w_s.at[e], w_r.at[slot], row_dev(e)
        )

    near = [(o, k2) for o in (1, 3) for k2 in range(2)]

    def near_row(o, k2):
        return lax.rem(z + o, 4) * 2 + k2

    def w_start(e):
        w_copy(e, my_row).start()
        sends.append(lambda: w_copy(e, my_row).wait_send())

    for o, k2 in near:
        w_start(near_row(o, k2))
    w_start(z * 2 + ek)
    arrivals["w_near"] = [lambda e=near_row(o, k2): w_copy(e, e).wait_recv() for o, k2 in near]
    arrivals["w"] = [lambda: w_copy(z * 2 + ek, z * 2 + ek).wait_recv()]
    keep("w", local(w_own.at[k], w_all.at[my_row], 8))

    arrive("enc")
    arrive("resid")
    for h in range(2):
        arrive(f"enc_{h}")
        for b in (2 * h, 2 * h + 1):
            cols = pl.ds(b * 1024, 1024)
            part = enc_buf[0, :, cols].astype(F32)
            for i in range(1, 4):
                part = part + enc_buf[i, :, cols].astype(F32)
            ez_own[:, cols] = part.astype(BF16)
        cols = pl.ds(h * 2048, 2048)
        ez = remote(ez_own.at[:, cols], ez_recv.at[:, cols], ez_s.at[h], ez_r.at[h], device(x, z, k, el, y))
        pair(f"ez_{h}", ez, ez)
    for name, l2, c in early:
        qg_start(name, l2, c)
    arrive("ez_0")
    arrive("ez_1")
    arrive("w_near")

    def w_pass(i):
        o = (3, 1)[i]
        part = w_all.at[pl.ds(lax.rem(z + o, 4) * 2, 2), pl.ds(64 * i, 64)]
        return remote(part, part, wf_s.at[i], wf_r.at[i], device(x, lax.rem(z + 4 - o, 4), k, l, y))

    def w_passed(i):
        part = w_all.at[pl.ds(lax.rem(z + 2, 4) * 2, 2), pl.ds(64 * i, 64)]
        return remote(part, part, wf_s.at[i], wf_r.at[i], device(x, lax.rem(z + 1, 4), k, l, y))

    for i in range(2):
        pair(f"w_far{i}", w_pass(i), w_passed(i))


    def hidden(b):
        cols = pl.ds(b * 1024, 1024)
        return (ez_own[:, cols].astype(F32) + ez_recv[:, cols].astype(F32)) + res_buf[:, cols].astype(F32)

    total = jnp.zeros((32, 1), F32)
    for b in range(4):
        h = hidden(b)
        total = total + jnp.sum(h * h, axis=1, keepdims=True)
    inv = lax.rsqrt(total * (1.0 / 4096.0) + 1e-06)
    for b in range(4):
        text32[b] = (hidden(b) * inv * gain[:, pl.ds(b * 1024, 1024)]).astype(BF16)

    def t1_copy(x2, slot):
        return remote(
            text32.at[x2], text.at[k, slot, rows_of(y, 32)], t1_s.at[x2], t1_r.at[slot], device(x2, z, k, l, y)
        )

    group("t1", 4, x, t1_copy)
    arrivals.pop("t1")
    keep("t1", local(text32.at[x], text.at[k, x, rows_of(y, 32)], 9))

    def t2_copy(x2, y2, slot):
        part = text.at[k, x2, rows_of(slot, 32)]
        return remote(part, part, t2_s.at[x2, y2], t2_r.at[x2, slot], y_dev(y2))

    order = (0, 2, 1, 3)
    for o in order:
        x2 = lax.rem(x + o, 4)
        if o == 0:
            arrive("t1")
        else:
            t1_copy(x2, x2).wait_recv()
        group(f"t2_{o}", 4, y, lambda y2, slot, x2=x2: t2_copy(x2, y2, slot))
    for name, l2, c in late:
        qg_start(name, l2, c)

    def t3_copy(core, x2):
        part = text.at[core, x2]
        return remote(part, part, t3_s.at[x2], t3_r.at[x2], device(x, z, ek, l, y))

    def kv_copy(c, e, slot):
        cols = pl.ds(CUTS[c][0], CUTS[c][1] - CUTS[c][0])
        return remote(
            kv_part.at[lax.div(e, 4), lax.rem(e, 4), :, cols],
            kv_recv.at[lax.div(slot, 4), lax.rem(slot, 4), :, cols],
            kv_s.at[c, e], kv_r.at[c, slot], clip_dev(e),
        )

    def project(x2):
        t = text[:, x2].reshape(256, 1024)
        for lo, hi in ((0, 256), (256, 640)):
            acc = dot(t, w_all[:, :, lo:hi].reshape(1024, hi - lo), 1, 0)
            kv_part[:, x2, :, lo:hi] = acc.astype(BF16).reshape(2, 128, hi - lo)

    def kv_start(c, core, x2):
        e = core * 4 + x2
        kv_copy(c, e, my_clip).start()
        sends.append(lambda: kv_copy(c, e, my_clip).wait_send())

    def kv_block(c, o):
        x2 = lax.rem(x + o, 4)
        cols = pl.ds(CUTS[c][0], CUTS[c][1] - CUTS[c][0])
        if o == 0:
            keep(f"kv{c}", local(kv_part.at[k, x, :, cols], kv_recv.at[k, x, :, cols], 14 + 2 * len(CUTS) + c))
        else:
            kv_start(c, k, x2)
        kv_start(c, ek, x2)

    held_parts = range(1, len(CUTS))
    held = []
    for o in order:
        x2 = lax.rem(x + o, 4)
        arrive(f"t2_{o}")
        pair(f"t3_{o}", t3_copy(k, x2), t3_copy(ek, x2))
        if o == 0:
            arrive("w")
            arrive("w_far0")
            arrive("w_far1")
        arrive(f"t3_{o}")
        project(x2)
        kv_block(0, o)
        for c in held_parts:
            held.append((c, o))
        if len(held) > HOLD * len(held_parts):
            for c, o2 in held[: len(held_parts)]:
                kv_block(c, o2)
            held = held[len(held_parts) :]
    for c, o2 in sorted(held):
        kv_block(c, o2)
    for c in range(len(CUTS)):
        arrivals[f"kv{c}"].append(lambda c=c: others(8, my_clip, lambda e: kv_copy(c, e, e).wait_recv()))

    def turn(z2):
        text_t[z2] = text[:, :, :, rows_of(z2, 256)].reshape(1024, 256).T

    each(0, 4, turn)

    def kx_copy(c, slot):
        part = kv.at[slot, :, :, pl.ds(CUTS[c][0], CUTS[c][1] - CUTS[c][0])]
        return remote(part, part, kx_s.at[c], kx_r.at[c], device(x, z, k, el, y))

    def gather_kv(c):
        lo, hi = CUTS[c]
        arrive(f"kv{c}")
        for i in range(2):
            acc = kv_recv[i, 0, :, lo:hi].astype(F32)
            for b in range(1, 4):
                acc = acc + kv_recv[i, b, :, lo:hi].astype(F32)
            kv[l, i, :, lo:hi] = acc.astype(BF16)
        pair(f"kx{c}", kx_copy(c, l), kx_copy(c, el))

    scale = HEAD ** (-0.5)

    def head(l2, c, keep):
        cols = pl.ds(pl.multiple_of(c * HEAD, HEAD), HEAD)
        qh, gh = q_buf[l2, :, cols], g_buf[l2, :, cols]
        kh, vh = kv[l2, 0, :, cols], kv[l2, 1, :, cols]
        e = jnp.exp(dot(kh, qh, 1, 1) * scale)
        probs = e * (1.0 / jnp.sum(e, axis=0, keepdims=True))
        probs_b = probs.astype(BF16)
        dprobs = dot(vh, gh, 1, 1)
        delta = jnp.sum(probs_b.astype(F32) * dprobs, axis=0, keepdims=True)
        ds = (probs * (dprobs - delta)).astype(BF16)
        qg_buf[l2, :, cols] = (dot(ds, kh, 0, 0) * scale).astype(BF16)
        keep[0, :, cols] = (dot(ds, qh, 1, 0) * scale).astype(keep.dtype)
        keep[1, :, cols] = dot(probs_b, gh, 1, 0).astype(keep.dtype)

    def heads(l2, c, keep):
        lo, hi = CUTS[c]
        each(lo // HEAD, hi // HEAD, lambda h: head(l2, h, keep))

    def px_start(c):
        lo, hi = CUTS[c]
        cols = pl.ds(lo, hi - lo)
        copy = remote(
            pg_send.at[:, :, cols], pg_recv.at[:, :, cols], px_s.at[c], px_r.at[c], device(x, z, k, el, y)
        )
        pair(f"px{c}", copy, copy)

    def oq_copy(l2, y2, slot):
        return remote(
            qg_buf.at[l2, rows_of(y2, 128)], out_q.at[0, :, columns(l2 * 4 + slot)],
            oq_s.at[l2, y2], oq_r.at[l2, slot], y_dev(y2),
        )

    def oq_start(name, l2, i):
        group(name, 4, y, lambda y2, slot: oq_copy(l2, y2, slot))
        keep(name, local(qg_buf.at[l2, rows_of(y, 128)], out_q.at[0, :, columns(l2 * 4 + y)], i))

    def ga_copy(c, e, slot):
        cols = pl.ds(CUTS[c][0], CUTS[c][1] - CUTS[c][0])
        return remote(
            gr_own.at[lax.div(e, 4), :, cols], gr_all.at[lax.div(slot, 4), lax.rem(slot, 4), :, cols],
            ga_s.at[c, e], ga_r.at[c, slot], clip_dev(e),
        )

    def ga_start(c):
        lo, hi = CUTS[c]
        cols = pl.ds(lo, hi - lo)
        arrive(f"px{c}")
        gr_own[:, :, lo:hi] = (pg_own[:, :, lo:hi] + pg_recv[:, :, lo:hi].astype(F32)).astype(BF16)
        group(f"ga{c}", 8, my_clip, lambda e, slot: ga_copy(c, e, slot))
        keep(f"ga{c}", local(gr_own.at[k, :, cols], gr_all.at[k, x, :, cols], 14 + c))

    def dw_copy(c, e, slot):
        cols = pl.ds(CUTS[c][0], CUTS[c][1] - CUTS[c][0])
        return remote(
            dw_part.at[e, :, cols], dw_recv.at[lax.rem(slot, 2), lax.div(slot, 2), :, cols],
            dw_s.at[c, e], dw_r.at[c, slot], row_dev(e),
        )

    def dw_send(c, e):
        dw_copy(c, e, my_row).start()
        sends.append(lambda: dw_copy(c, e, my_row).wait_send())

    def dw_pass(c, i):
        cols = pl.ds(CUTS[c][0], CUTS[c][1] - CUTS[c][0])
        return remote(
            dw_part.at[lax.rem(z + 2, 4) * 2 + i, :, cols], dw_mid.at[i, :, cols],
            dp_s.at[c, i], dp_r.at[c, i], device(x, lax.rem(z + (1, 3)[i], 4), k, l, y),
        )

    def dw_start(c):
        lo, hi = CUTS[c]
        cols = pl.ds(lo, hi - lo)
        arrive(f"ga{c}")
        grads_c = gr_all[:, :, :, lo:hi].reshape(1024, hi - lo)

        def step(z2):
            acc = dot(text_t[z2], grads_c, 1, 0)
            dw_part[pl.ds(z2 * 2, 2), :, lo:hi] = acc.astype(BF16).reshape(2, 128, hi - lo)

        step(lax.rem(z + 2, 4))
        for i in range(2):
            pair(f"dp{c}{i}", dw_pass(c, i), dw_pass(c, i))
        for i, o in ((0, 1), (1, 3)):
            step(lax.rem(z + o, 4))
            dw_send(c, near_row(o, 1 - i))
        step(z)
        dw_send(c, z * 2 + ek)
        keep(f"dw{c}", local(dw_part.at[my_row, :, cols], dw_recv.at[k, z, :, cols], 14 + len(CUTS) + c))
        arrivals[f"dw{c}"] += [
            lambda e=e: dw_copy(c, e, e).wait_recv()
            for e in [near_row(o, k2) for o, k2 in near] + [z * 2 + ek]
        ]

    def dw_add(c):
        lo, hi = CUTS[c]
        for i, o in ((0, 1), (1, 3)):
            arrive(f"dp{c}{i}")
            e = near_row(o, i)
            both = dw_part[e, :, lo:hi].astype(F32) + dw_mid[i, :, lo:hi].astype(F32)
            dw_part[e, :, lo:hi] = both.astype(BF16)
            dw_send(c, e)

    def dw_end(c):
        lo, hi = CUTS[c]
        arrive(f"dw{c}")
        for i, out in ((0, out_k), (1, out_v)):
            acc = dw_recv[i, z, :, lo:hi].astype(F32)
            for o in (1, 3):
                acc = acc + dw_recv[i, lax.rem(z + o, 4), :, lo:hi].astype(F32)
            out[:, lo:hi] = acc

    last = len(CUTS) - 1
    arrive("mine")

    def heads_of(name, l2, c, kept):
        for i in range(2):
            arrive(f"{name}_{c}_{i}")
        heads(l2, c, kept)

    for c in range(len(CUTS)):
        gather_kv(c)
        heads_of("own", l, c, pg_own)
        if c > 0:
            ga_start(c - 1)
        arrive(f"kx{c}")
        heads_of("far", el, c, pg_send)
        px_start(c)
        if c == last:
            oq_start("oq_own", l, 12)
            oq_start("oq_far", el, 13)
            if last > 0:
                dw_start(0)
            ga_start(c)
    for c in range(len(CUTS)):
        if c > 0 or last == 0:
            dw_start(c)
        if c > 0:
            dw_add(c - 1)
    dw_add(last)
    for c in range(len(CUTS)):
        dw_end(c)
    flush()


def on_device(enc_terms, enc_resid, norm_gain, key_weight, value_weight, queries, out_grad):
    any_spec = pl.BlockSpec(memory_space=pl.ANY)
    vmem = pl.BlockSpec(memory_space=pltpu.VMEM)
    dma = pltpu.SemaphoreType.DMA
    n = len(CUTS)
    scratch = [
        pltpu.VMEM((4, 32, 4096), BF16),
        pltpu.VMEM((32, 4096), BF16),
        pltpu.VMEM((32, 4096), BF16),
        pltpu.VMEM((32, 4096), BF16),
        pltpu.VMEM((4, 32, 1024), BF16),
        pltpu.VMEM((2, 4, 128, 1024), BF16),
        pltpu.VMEM((4, 256, 1024), BF16),
        pltpu.VMEM((2, 128, 640), BF16),
        pltpu.VMEM((8, 128, 640), BF16),
        pltpu.VMEM((2, 4, 128, 640), BF16),
        pltpu.VMEM((2, 4, 128, 640), BF16),
        pltpu.VMEM((2, 2, 128, 640), BF16),
        pltpu.VMEM((2, 512, 640), BF16),
        pltpu.VMEM((2, 512, 640), BF16),
        pltpu.VMEM((2, 512, 640), BF16),
        pltpu.VMEM((2, 128, 640), BF16),
        pltpu.VMEM((2, 128, 640), F32),
        pltpu.VMEM((2, 128, 640), BF16),
        pltpu.VMEM((2, 128, 640), BF16),
        pltpu.VMEM((2, 4, 128, 640), BF16),
        pltpu.VMEM((8, 128, 640), BF16),
        pltpu.VMEM((2, 4, 128, 640), BF16),
        pltpu.VMEM((2, 128, 640), BF16),
        dma((14 + 3 * n,)),
        dma((2, 4)), dma((2, 4)),
        dma((2,)), dma((2,)),
        dma((4,)), dma((4,)),
        dma((4, 4)), dma((4, 4)),
        dma((4,)), dma((4,)),
        dma((8,)), dma((8,)),
        dma((2,)), dma((2,)),
        dma((n, 8)), dma((n, 8)),
        dma((n,)), dma((n,)),
        dma((2, 2, n, 4)), dma((2, 2, n, 4)),
        dma((n,)), dma((n,)),
        dma((2, 4)), dma((2, 4)),
        dma((n, 8)), dma((n, 8)),
        dma((n, 8)), dma((n, 8)),
        dma((n, 2)), dma((n, 2)),
    ]
    return pl.pallas_call(
        kernel,
        out_shape=(
            jax.ShapeDtypeStruct(queries.shape, BF16),
            jax.ShapeDtypeStruct(key_weight.shape, F32),
            jax.ShapeDtypeStruct(value_weight.shape, F32),
        ),
        in_specs=[any_spec, any_spec, vmem, any_spec, any_spec, any_spec, any_spec],
        out_specs=(any_spec, vmem, vmem),
        scratch_shapes=scratch,
        compiler_params=pltpu.CompilerParams(
            collective_id=0, has_side_effects=True, vmem_limit_bytes=62 * 2**20
        ),
        cost_estimate=pl.CostEstimate(flops=4 * 10**9, bytes_accessed=10**7, transcendentals=655360),
    )(enc_terms, enc_resid, norm_gain.reshape(1, -1), key_weight, value_weight, queries, out_grad)


def solution(mesh):
    in_specs = (
        P("clip", "seq", None, None),
        P("clip", None, None),
        P(),
        P("clip", "seq"),
        P("clip", "seq"),
        P("clip", "seq", None),
        P("clip", "seq", None),
    )
    out_specs = (P("clip", "seq", None), P("clip", "seq"), P("clip", "seq"))
    return jax.shard_map(
        on_device, mesh=mesh, in_specs=in_specs, out_specs=out_specs, check_vma=False
    )
```

```python
import jax
import jax.numpy as jnp
from jax import lax
from jax.experimental import pallas as pl
from jax.experimental.pallas import tpu as pltpu
from jax.sharding import PartitionSpec as P

MESH = pl.DeviceIdType.MESH
HEAD = 128
F32 = jnp.float32
BF16 = jnp.bfloat16
CUTS = ((0, 128), (128, 384), (384, 640))
EARLY = 2
HOLD = 0


def dot(a, b, ca, cb):
    return lax.dot_general(a, b, (((ca,), (cb,)), ((), ())), preferred_element_type=F32)


def each(start, stop, body):
    lax.fori_loop(start, stop, lambda i, c: (body(i), c)[1], 0)


def device(x, z, k, l, y):
    return ((x * 4 + z) * 2 + k, l * 4 + y)


def kernel(
    enc, resid, gain, key_w, val_w, queries, grads,
    out_q, out_k, out_v,
    enc_buf, res_buf, ez_own, ez_recv, text32, text, text_t, w_own, w_all, kv_part, kv_recv, kv, q_buf, g_buf, qg_buf,
    pg_send, pg_own, pg_recv, gr_own, gr_all, dw_part, dw_recv, dw_mid,
    loc, e_s, e_r, ez_s, ez_r, t1_s, t1_r, t2_s, t2_r, t3_s, t3_r, w_s, w_r, wf_s, wf_r, kv_s, kv_r, kx_s, kx_r,
    qg_s, qg_r, px_s, px_r, oq_s, oq_r, ga_s, ga_r, dw_s, dw_r, dp_s, dp_r,
):
    clip, seq = lax.axis_index("clip"), lax.axis_index("seq")
    x, z, k = lax.div(clip, 8), lax.rem(lax.div(clip, 2), 4), lax.rem(clip, 2)
    l, y = lax.div(seq, 4), lax.rem(seq, 4)
    el, ek = 1 - l, 1 - k
    my_row, my_clip = z * 2 + k, k * 4 + x

    def y_dev(y2):
        return device(x, z, k, l, y2)

    def row_dev(e):
        return device(x, lax.div(e, 2), lax.rem(e, 2), l, y)

    def clip_dev(e):
        return device(lax.rem(e, 4), z, lax.div(e, 4), l, y)

    def others(n, me, body):
        each(1, n, lambda o: body(lax.rem(me + o, n)))

    def remote(src, dst, s, r, where):
        return pltpu.make_async_remote_copy(
            src_ref=src, dst_ref=dst, send_sem=s, recv_sem=r, device_id=where, device_id_type=MESH
        )

    def local(src, dst, i):
        return pltpu.make_async_copy(src, dst, loc.at[i])

    sends, arrivals = [], {}

    def arrive(name):
        for wait in arrivals.pop(name):
            wait()

    def flush():
        for name in list(arrivals):
            arrive(name)
        for wait in sends:
            wait()

    def group(name, n, me, copy):
        others(n, me, lambda e: copy(e, me).start())
        sends.append(lambda: others(n, me, lambda e: copy(e, me).wait_send()))
        arrivals[name] = [lambda: others(n, me, lambda e: copy(e, e).wait_recv())]

    def pair(name, copy, back):
        copy.start()
        sends.append(copy.wait_send)
        arrivals[name] = [back.wait_recv]

    def keep(name, copy):
        copy.start()
        arrivals.setdefault(name, []).append(copy.wait)

    def rows_of(i, n):
        return pl.ds(pl.multiple_of(i * n, n), n)

    def columns(j):
        return pl.ds(pl.multiple_of(j * 640, 128), 640)

    keep("enc", local(enc.at[0, 0, rows_of(y, 32)], enc_buf.at[y], 0))
    keep("resid", local(resid.at[0, rows_of(y, 32)], res_buf, 1))
    keep("w_own", local(key_w, w_own.at[0], 2))
    keep("w_own", local(val_w, w_own.at[1], 3))

    def qg_copy(i, l2, c, y2, slot):
        src, dst = ((queries, q_buf), (grads, g_buf))[i]
        lo, hi = CUTS[c]
        return remote(
            src.at[0, :, pl.ds(pl.multiple_of((l2 * 4 + y2) * 640 + lo, 128), hi - lo)],
            dst.at[l2, rows_of(slot, 128), pl.ds(lo, hi - lo)],
            qg_s.at[i, l2, c, y2], qg_r.at[i, l2, c, slot], y_dev(y2),
        )

    def qg_own(i, l2):
        src, dst = ((queries, q_buf), (grads, g_buf))[i]
        return local(src.at[0, :, columns(l2 * 4 + y)], dst.at[l2, rows_of(y, 128)], 4 + 2 * i + l2)

    def qg_start(name, l2, c):
        for i in range(2):
            group(f"{name}_{c}_{i}", 4, y, lambda y2, slot, i=i: qg_copy(i, l2, c, y2, slot))

    pieces = [p for c in range(len(CUTS)) for p in (("own", l, c), ("far", el, c))]
    early, late = pieces[:EARLY], pieces[EARLY:]
    for i in range(2):
        keep("mine", qg_own(i, 0))
        keep("mine", qg_own(i, 1))

    bar = pltpu.get_barrier_semaphore()

    def greet(where):
        pl.semaphore_signal(bar, inc=1, device_id=where, device_id_type=MESH)

    others(4, y, lambda e: greet(y_dev(e)))
    greet(device(x, z, k, el, y))
    for o in (1, 3):
        for k2 in range(2):
            greet(device(x, lax.rem(z + o, 4), k2, l, y))
    greet(device(x, z, ek, l, y))
    others(8, my_clip, lambda e: greet(clip_dev(e)))
    pl.semaphore_wait(bar, 16)

    def enc_copy(h, y2, slot):
        cols = pl.ds(h * 2048, 2048)
        return remote(
            enc.at[0, 0, rows_of(y2, 32), cols], enc_buf.at[slot, :, cols], e_s.at[h, y2], e_r.at[h, slot], y_dev(y2)
        )

    group("enc_0", 4, y, lambda y2, slot: enc_copy(0, y2, slot))
    group("enc_1", 4, y, lambda y2, slot: enc_copy(1, y2, slot))

    arrive("w_own")

    def w_copy(e, slot):
        return remote(
            w_own.at[lax.rem(e, 2)], w_all.at[slot], w_s.at[e], w_r.at[slot], row_dev(e)
        )

    near = [(o, k2) for o in (1, 3) for k2 in range(2)]

    def near_row(o, k2):
        return lax.rem(z + o, 4) * 2 + k2

    def w_start(e):
        w_copy(e, my_row).start()
        sends.append(lambda: w_copy(e, my_row).wait_send())

    for o, k2 in near:
        w_start(near_row(o, k2))
    w_start(z * 2 + ek)
    arrivals["w_near"] = [lambda e=near_row(o, k2): w_copy(e, e).wait_recv() for o, k2 in near]
    arrivals["w"] = [lambda: w_copy(z * 2 + ek, z * 2 + ek).wait_recv()]
    keep("w", local(w_own.at[k], w_all.at[my_row], 8))

    arrive("enc")
    arrive("resid")
    for h in range(2):
        arrive(f"enc_{h}")
        for b in (2 * h, 2 * h + 1):
            cols = pl.ds(b * 1024, 1024)
            part = enc_buf[0, :, cols].astype(F32)
            for i in range(1, 4):
                part = part + enc_buf[i, :, cols].astype(F32)
            ez_own[:, cols] = part.astype(BF16)
        cols = pl.ds(h * 2048, 2048)
        ez = remote(ez_own.at[:, cols], ez_recv.at[:, cols], ez_s.at[h], ez_r.at[h], device(x, z, k, el, y))
        pair(f"ez_{h}", ez, ez)
    for name, l2, c in early:
        qg_start(name, l2, c)
    arrive("ez_0")
    arrive("ez_1")
    arrive("w_near")

    def w_pass(i):
        o = (3, 1)[i]
        part = w_all.at[pl.ds(lax.rem(z + o, 4) * 2, 2), pl.ds(64 * i, 64)]
        return remote(part, part, wf_s.at[i], wf_r.at[i], device(x, lax.rem(z + 4 - o, 4), k, l, y))

    def w_passed(i):
        part = w_all.at[pl.ds(lax.rem(z + 2, 4) * 2, 2), pl.ds(64 * i, 64)]
        return remote(part, part, wf_s.at[i], wf_r.at[i], device(x, lax.rem(z + 1, 4), k, l, y))

    for i in range(2):
        pair(f"w_far{i}", w_pass(i), w_passed(i))


    def hidden(b):
        cols = pl.ds(b * 1024, 1024)
        return (ez_own[:, cols].astype(F32) + ez_recv[:, cols].astype(F32)) + res_buf[:, cols].astype(F32)

    total = jnp.zeros((32, 1), F32)
    for b in range(4):
        h = hidden(b)
        total = total + jnp.sum(h * h, axis=1, keepdims=True)
    inv = lax.rsqrt(total * (1.0 / 4096.0) + 1e-06)
    for b in range(4):
        text32[b] = (hidden(b) * inv * gain[:, pl.ds(b * 1024, 1024)]).astype(BF16)

    def t1_copy(x2, slot):
        return remote(
            text32.at[x2], text.at[k, slot, rows_of(y, 32)], t1_s.at[x2], t1_r.at[slot], device(x2, z, k, l, y)
        )

    group("t1", 4, x, t1_copy)
    arrivals.pop("t1")
    keep("t1", local(text32.at[x], text.at[k, x, rows_of(y, 32)], 9))

    def t2_copy(x2, y2, slot):
        part = text.at[k, x2, rows_of(slot, 32)]
        return remote(part, part, t2_s.at[x2, y2], t2_r.at[x2, slot], y_dev(y2))

    order = (0, 2, 1, 3)
    for o in order:
        x2 = lax.rem(x + o, 4)
        if o == 0:
            arrive("t1")
        else:
            t1_copy(x2, x2).wait_recv()
        group(f"t2_{o}", 4, y, lambda y2, slot, x2=x2: t2_copy(x2, y2, slot))
    for name, l2, c in late:
        qg_start(name, l2, c)

    def t3_copy(core, x2):
        part = text.at[core, x2]
        return remote(part, part, t3_s.at[x2], t3_r.at[x2], device(x, z, ek, l, y))

    def kv_copy(c, e, slot):
        cols = pl.ds(CUTS[c][0], CUTS[c][1] - CUTS[c][0])
        return remote(
            kv_part.at[lax.div(e, 4), lax.rem(e, 4), :, cols],
            kv_recv.at[lax.div(slot, 4), lax.rem(slot, 4), :, cols],
            kv_s.at[c, e], kv_r.at[c, slot], clip_dev(e),
        )

    def project(x2):
        t = text[:, x2].reshape(256, 1024)
        for lo, hi in ((0, 256), (256, 640)):
            acc = dot(t, w_all[:, :, lo:hi].reshape(1024, hi - lo), 1, 0)
            kv_part[:, x2, :, lo:hi] = acc.astype(BF16).reshape(2, 128, hi - lo)

    def kv_start(c, core, x2):
        e = core * 4 + x2
        kv_copy(c, e, my_clip).start()
        sends.append(lambda: kv_copy(c, e, my_clip).wait_send())

    def kv_block(c, o):
        x2 = lax.rem(x + o, 4)
        cols = pl.ds(CUTS[c][0], CUTS[c][1] - CUTS[c][0])
        if o == 0:
            keep(f"kv{c}", local(kv_part.at[k, x, :, cols], kv_recv.at[k, x, :, cols], 14 + 2 * len(CUTS) + c))
        else:
            kv_start(c, k, x2)
        kv_start(c, ek, x2)

    held_parts = range(1, len(CUTS))
    held = []
    for o in order:
        x2 = lax.rem(x + o, 4)
        arrive(f"t2_{o}")
        pair(f"t3_{o}", t3_copy(k, x2), t3_copy(ek, x2))
        if o == 0:
            arrive("w")
            arrive("w_far0")
            arrive("w_far1")
        arrive(f"t3_{o}")
        project(x2)
        kv_block(0, o)
        for c in held_parts:
            held.append((c, o))
        if len(held) > HOLD * len(held_parts):
            for c, o2 in held[: len(held_parts)]:
                kv_block(c, o2)
            held = held[len(held_parts) :]
    for c, o2 in sorted(held):
        kv_block(c, o2)
    for c in range(len(CUTS)):
        arrivals[f"kv{c}"].append(lambda c=c: others(8, my_clip, lambda e: kv_copy(c, e, e).wait_recv()))

    def turn(z2):
        text_t[z2] = text[:, :, :, rows_of(z2, 256)].reshape(1024, 256).T

    each(0, 4, turn)

    def kx_copy(c, slot):
        part = kv.at[slot, :, :, pl.ds(CUTS[c][0], CUTS[c][1] - CUTS[c][0])]
        return remote(part, part, kx_s.at[c], kx_r.at[c], device(x, z, k, el, y))

    def gather_kv(c):
        lo, hi = CUTS[c]
        arrive(f"kv{c}")
        for i in range(2):
            acc = kv_recv[i, 0, :, lo:hi].astype(F32)
            for b in range(1, 4):
                acc = acc + kv_recv[i, b, :, lo:hi].astype(F32)
            kv[l, i, :, lo:hi] = acc.astype(BF16)
        pair(f"kx{c}", kx_copy(c, l), kx_copy(c, el))

    scale = HEAD ** (-0.5)

    def head(l2, c, keep):
        cols = pl.ds(pl.multiple_of(c * HEAD, HEAD), HEAD)
        qh, gh = q_buf[l2, :, cols], g_buf[l2, :, cols]
        kh, vh = kv[l2, 0, :, cols], kv[l2, 1, :, cols]
        e = jnp.exp(dot(kh, qh, 1, 1) * scale)
        probs = e * (1.0 / jnp.sum(e, axis=0, keepdims=True))
        probs_b = probs.astype(BF16)
        dprobs = dot(vh, gh, 1, 1)
        delta = jnp.sum(probs_b.astype(F32) * dprobs, axis=0, keepdims=True)
        ds = (probs * (dprobs - delta)).astype(BF16)
        qg_buf[l2, :, cols] = (dot(ds, kh, 0, 0) * scale).astype(BF16)
        keep[0, :, cols] = (dot(ds, qh, 1, 0) * scale).astype(keep.dtype)
        keep[1, :, cols] = dot(probs_b, gh, 1, 0).astype(keep.dtype)

    def heads(l2, c, keep):
        lo, hi = CUTS[c]
        each(lo // HEAD, hi // HEAD, lambda h: head(l2, h, keep))

    def px_start(c):
        lo, hi = CUTS[c]
        cols = pl.ds(lo, hi - lo)
        copy = remote(
            pg_send.at[:, :, cols], pg_recv.at[:, :, cols], px_s.at[c], px_r.at[c], device(x, z, k, el, y)
        )
        pair(f"px{c}", copy, copy)

    def oq_copy(l2, y2, slot):
        return remote(
            qg_buf.at[l2, rows_of(y2, 128)], out_q.at[0, :, columns(l2 * 4 + slot)],
            oq_s.at[l2, y2], oq_r.at[l2, slot], y_dev(y2),
        )

    def oq_start(name, l2, i):
        group(name, 4, y, lambda y2, slot: oq_copy(l2, y2, slot))
        keep(name, local(qg_buf.at[l2, rows_of(y, 128)], out_q.at[0, :, columns(l2 * 4 + y)], i))

    def ga_copy(c, e, slot):
        cols = pl.ds(CUTS[c][0], CUTS[c][1] - CUTS[c][0])
        return remote(
            gr_own.at[lax.div(e, 4), :, cols], gr_all.at[lax.div(slot, 4), lax.rem(slot, 4), :, cols],
            ga_s.at[c, e], ga_r.at[c, slot], clip_dev(e),
        )

    def ga_start(c):
        lo, hi = CUTS[c]
        cols = pl.ds(lo, hi - lo)
        arrive(f"px{c}")
        gr_own[:, :, lo:hi] = (pg_own[:, :, lo:hi] + pg_recv[:, :, lo:hi].astype(F32)).astype(BF16)
        group(f"ga{c}", 8, my_clip, lambda e, slot: ga_copy(c, e, slot))
        keep(f"ga{c}", local(gr_own.at[k, :, cols], gr_all.at[k, x, :, cols], 14 + c))

    def dw_copy(c, e, slot):
        cols = pl.ds(CUTS[c][0], CUTS[c][1] - CUTS[c][0])
        return remote(
            dw_part.at[e, :, cols], dw_recv.at[lax.rem(slot, 2), lax.div(slot, 2), :, cols],
            dw_s.at[c, e], dw_r.at[c, slot], row_dev(e),
        )

    def dw_send(c, e):
        dw_copy(c, e, my_row).start()
        sends.append(lambda: dw_copy(c, e, my_row).wait_send())

    def dw_pass(c, i):
        cols = pl.ds(CUTS[c][0], CUTS[c][1] - CUTS[c][0])
        return remote(
            dw_part.at[lax.rem(z + 2, 4) * 2 + i, :, cols], dw_mid.at[i, :, cols],
            dp_s.at[c, i], dp_r.at[c, i], device(x, lax.rem(z + (1, 3)[i], 4), k, l, y),
        )

    def dw_start(c):
        lo, hi = CUTS[c]
        cols = pl.ds(lo, hi - lo)
        arrive(f"ga{c}")
        grads_c = gr_all[:, :, :, lo:hi].reshape(1024, hi - lo)

        def step(z2):
            acc = dot(text_t[z2], grads_c, 1, 0)
            dw_part[pl.ds(z2 * 2, 2), :, lo:hi] = acc.astype(BF16).reshape(2, 128, hi - lo)

        step(lax.rem(z + 2, 4))
        for i in range(2):
            pair(f"dp{c}{i}", dw_pass(c, i), dw_pass(c, i))
        for i, o in ((0, 1), (1, 3)):
            step(lax.rem(z + o, 4))
            dw_send(c, near_row(o, 1 - i))
        step(z)
        dw_send(c, z * 2 + ek)
        keep(f"dw{c}", local(dw_part.at[my_row, :, cols], dw_recv.at[k, z, :, cols], 14 + len(CUTS) + c))
        arrivals[f"dw{c}"] += [
            lambda e=e: dw_copy(c, e, e).wait_recv()
            for e in [near_row(o, k2) for o, k2 in near] + [z * 2 + ek]
        ]

    def dw_add(c):
        lo, hi = CUTS[c]
        for i, o in ((0, 1), (1, 3)):
            arrive(f"dp{c}{i}")
            e = near_row(o, i)
            both = dw_part[e, :, lo:hi].astype(F32) + dw_mid[i, :, lo:hi].astype(F32)
            dw_part[e, :, lo:hi] = both.astype(BF16)
            dw_send(c, e)

    def dw_end(c):
        lo, hi = CUTS[c]
        arrive(f"dw{c}")
        for i, out in ((0, out_k), (1, out_v)):
            acc = dw_recv[i, z, :, lo:hi].astype(F32)
            for o in (1, 3):
                acc = acc + dw_recv[i, lax.rem(z + o, 4), :, lo:hi].astype(F32)
            out[:, lo:hi] = acc

    last = len(CUTS) - 1
    arrive("mine")

    def heads_of(name, l2, c, kept):
        for i in range(2):
            arrive(f"{name}_{c}_{i}")
        heads(l2, c, kept)

    for c in range(len(CUTS)):
        gather_kv(c)
        heads_of("own", l, c, pg_own)
        if c > 0:
            ga_start(c - 1)
        arrive(f"kx{c}")
        heads_of("far", el, c, pg_send)
        px_start(c)
        if c == last:
            if last > 0:
                dw_start(0)
            ga_start(c)
            oq_start("oq_own", l, 12)
            oq_start("oq_far", el, 13)
    for c in range(len(CUTS)):
        if c > 0 or last == 0:
            dw_start(c)
        if c > 0:
            dw_add(c - 1)
    dw_add(last)
    for c in range(len(CUTS)):
        dw_end(c)
    flush()


def on_device(enc_terms, enc_resid, norm_gain, key_weight, value_weight, queries, out_grad):
    any_spec = pl.BlockSpec(memory_space=pl.ANY)
    vmem = pl.BlockSpec(memory_space=pltpu.VMEM)
    dma = pltpu.SemaphoreType.DMA
    n = len(CUTS)
    scratch = [
        pltpu.VMEM((4, 32, 4096), BF16),
        pltpu.VMEM((32, 4096), BF16),
        pltpu.VMEM((32, 4096), BF16),
        pltpu.VMEM((32, 4096), BF16),
        pltpu.VMEM((4, 32, 1024), BF16),
        pltpu.VMEM((2, 4, 128, 1024), BF16),
        pltpu.VMEM((4, 256, 1024), BF16),
        pltpu.VMEM((2, 128, 640), BF16),
        pltpu.VMEM((8, 128, 640), BF16),
        pltpu.VMEM((2, 4, 128, 640), BF16),
        pltpu.VMEM((2, 4, 128, 640), BF16),
        pltpu.VMEM((2, 2, 128, 640), BF16),
        pltpu.VMEM((2, 512, 640), BF16),
        pltpu.VMEM((2, 512, 640), BF16),
        pltpu.VMEM((2, 512, 640), BF16),
        pltpu.VMEM((2, 128, 640), BF16),
        pltpu.VMEM((2, 128, 640), F32),
        pltpu.VMEM((2, 128, 640), BF16),
        pltpu.VMEM((2, 128, 640), BF16),
        pltpu.VMEM((2, 4, 128, 640), BF16),
        pltpu.VMEM((8, 128, 640), BF16),
        pltpu.VMEM((2, 4, 128, 640), BF16),
        pltpu.VMEM((2, 128, 640), BF16),
        dma((14 + 3 * n,)),
        dma((2, 4)), dma((2, 4)),
        dma((2,)), dma((2,)),
        dma((4,)), dma((4,)),
        dma((4, 4)), dma((4, 4)),
        dma((4,)), dma((4,)),
        dma((8,)), dma((8,)),
        dma((2,)), dma((2,)),
        dma((n, 8)), dma((n, 8)),
        dma((n,)), dma((n,)),
        dma((2, 2, n, 4)), dma((2, 2, n, 4)),
        dma((n,)), dma((n,)),
        dma((2, 4)), dma((2, 4)),
        dma((n, 8)), dma((n, 8)),
        dma((n, 8)), dma((n, 8)),
        dma((n, 2)), dma((n, 2)),
    ]
    return pl.pallas_call(
        kernel,
        out_shape=(
            jax.ShapeDtypeStruct(queries.shape, BF16),
            jax.ShapeDtypeStruct(key_weight.shape, F32),
            jax.ShapeDtypeStruct(value_weight.shape, F32),
        ),
        in_specs=[any_spec, any_spec, vmem, any_spec, any_spec, any_spec, any_spec],
        out_specs=(any_spec, vmem, vmem),
        scratch_shapes=scratch,
        compiler_params=pltpu.CompilerParams(
            collective_id=0, has_side_effects=True, vmem_limit_bytes=62 * 2**20
        ),
        cost_estimate=pl.CostEstimate(flops=4 * 10**9, bytes_accessed=10**7, transcendentals=655360),
    )(enc_terms, enc_resid, norm_gain.reshape(1, -1), key_weight, value_weight, queries, out_grad)


def solution(mesh):
    in_specs = (
        P("clip", "seq", None, None),
        P("clip", None, None),
        P(),
        P("clip", "seq"),
        P("clip", "seq"),
        P("clip", "seq", None),
        P("clip", "seq", None),
    )
    out_specs = (P("clip", "seq", None), P("clip", "seq"), P("clip", "seq"))
    return jax.shard_map(
        on_device, mesh=mesh, in_specs=in_specs, out_specs=out_specs, check_vma=False
    )
```
